32 devices in a mesh: alpha: 8 (over z, y), beta: 4 (over x, core).
Axes of the slice: x: 2, y: 2, z: 4, core: 2. Of those that a mesh axis runs over, the one named last changes fastest.
Arguments:
- ci_vector: float32 [1024, 1024], P('alpha', 'beta'), may hold values from -6 to 6
- one_body: float32 [102], replicated, may hold values from -1 to 1
- pair_integrals: bfloat16 [102, 102], replicated, may hold values from -0.15625 to 0.15625
- beta_target: int32 [40, 1024], P(None, 'beta'), may hold values from 0 to 1023
- beta_pair: int32 [40, 1024], P(None, 'beta'), may hold values from 0 to 101
- beta_sign: int32 [40, 1024], P(None, 'beta'), may hold values 0 or 1
- alpha_target: int32 [40, 1024], P(None, 'alpha'), may hold values from 0 to 1023
- alpha_pair: int32 [40, 1024], P(None, 'alpha'), may hold values from 0 to 101
- alpha_sign: int32 [40, 1024], P(None, 'alpha'), may hold values 0 or 1
Outputs:
- sigma_vector: float32 [1024, 1024], P('alpha', 'beta')
The draws below stay inside these ranges and needn't reach their ends.
All inputs are finite; a program needn't handle non-finite values. No bound on the sum of `beta_sign` or of `alpha_sign` on one device may be relied on, other than what follows from the above.
Results may differ from the reference program's by a relative error of at most 0.0035.
Values may be sent and summed in bfloat16 or wider, within the bound.
No kernel may reach another device: no remote copies, remote signals or barrier semaphores. Data moves between devices by JAX's collectives and lax.ppermute only.
A program may use at most 128 MiB of HBM per device.

```python
import jax
import jax.numpy as jnp
from jax import lax

NP = 102
NEXC = 40
NA = 1024
NB = 1024


def set_ends(result, stream_key, low, high):
    longest = result.shape.index(max(result.shape))
    spots = []
    for shift in (0, 1):
        where = [jax.random.randint(jax.random.fold_in(stream_key, axis), (), 0, length) for axis, length in enumerate(result.shape)]
        where[longest] = (where[longest] + shift) % result.shape[longest]
        spots.append(tuple(where))
    return result.at[spots[0]].set(low).at[spots[1]].set(high)


def steps_of(key, extent, shards, smallest, top_value):
    loudness, own = 1.0, jax.random.fold_in(key, 6)
    for position, blocks in shards:
        steps = jnp.exp(jax.random.uniform(jax.random.fold_in(own, position), (blocks,), jnp.float32, smallest / len(shards), top_value / len(shards)))
        loudness = loudness * jnp.repeat(steps, extent[position] // blocks).reshape([-1 if axis == position else 1 for axis in range(len(extent))])
    return loudness


def gaussian(stream_key, extent, width, most, split=(), kind=jnp.bfloat16):
    array = width * jax.random.normal(stream_key, extent, jnp.float32)
    if split:
        array = array * steps_of(stream_key, extent, split, -0.22, 0.18)
    return jnp.clip(array, -most, most).astype(kind)


def setup_inputs(seed: int = 0) -> dict:
    key_list = jax.random.split(jax.random.key(seed), 10)
    return {
        "ci_vector": gaussian(key_list[0], (NA, NB), 1.0, 6.0, ((0, 8), (1, 4)), jnp.float32),
        "one_body": gaussian(key_list[1], (NP,), NEXC ** -0.5, 1.0, (), jnp.float32),
        "pair_integrals": gaussian(key_list[2], (NP, NP), (NEXC * NEXC) ** -0.5, 0.15625),
        "beta_target": set_ends(jax.random.randint(key_list[3], (NEXC, NB), 0, NB), jax.random.fold_in(key_list[3], 1), 0, NB - 1).astype(jnp.int32),
        "beta_pair": set_ends(jax.random.randint(key_list[4], (NEXC, NB), 0, NP), jax.random.fold_in(key_list[4], 1), 0, NP - 1).astype(jnp.int32),
        "beta_sign": set_ends((jax.random.randint(key_list[5], (NEXC, NB), 0, 2) < 1).astype(jnp.int32), jax.random.fold_in(key_list[5], 1), 0, 1),
        "alpha_target": set_ends(jax.random.randint(key_list[6], (NEXC, NA), 0, NA), jax.random.fold_in(key_list[6], 1), 0, NA - 1).astype(jnp.int32),
        "alpha_pair": set_ends(jax.random.randint(key_list[7], (NEXC, NA), 0, NP), jax.random.fold_in(key_list[7], 1), 0, NP - 1).astype(jnp.int32),
        "alpha_sign": set_ends((jax.random.randint(key_list[8], (NEXC, NA), 0, 2) < 1).astype(jnp.int32), jax.random.fold_in(key_list[8], 1), 0, 1),
    }


precise = lax.Precision.HIGHEST


def reference(ci_vector, one_body, pair_integrals, beta_target, beta_pair, beta_sign, alpha_target, alpha_pair, alpha_sign):
    civec_bf = ci_vector.astype(jnp.bfloat16)
    civec_up = lax.optimization_barrier(civec_bf).astype(jnp.float32)
    pair_ids = jnp.arange(NP, dtype=jnp.int32)
    beta_hot = ((2 * beta_sign - 1)[:, :, None] * (beta_pair[:, :, None] == pair_ids).astype(jnp.int32)).astype(jnp.float32)
    alpha_hot = ((2 * alpha_sign - 1)[:, :, None] * (alpha_pair[:, :, None] == pair_ids).astype(jnp.int32)).astype(jnp.float32)
    alpha_level = jnp.einsum("eaq,q->ea", alpha_hot, one_body, precision=precise)
    integrals = pair_integrals.astype(jnp.float32)
    block_rows = 32

    def accumulate(sigma_out, block_index):
        offset = block_index * block_rows
        rows_here = lax.dynamic_slice_in_dim(civec_up, offset, block_rows, 0)
        picked = jnp.take(rows_here, beta_target, axis=1)
        density = jnp.einsum("aei,eip->pai", picked, beta_hot, precision=precise)
        same_beta = jnp.einsum("p,pai->ai", one_body, density, precision=precise)
        density_bf = lax.optimization_barrier(density.astype(jnp.bfloat16)).astype(jnp.float32)
        mixed = jnp.einsum("qp,pai->qai", integrals, density_bf, precision=precise)
        mixed_bf = lax.optimization_barrier(mixed.astype(jnp.bfloat16)).astype(jnp.float32)
        hot_rows = lax.dynamic_slice_in_dim(alpha_hot, offset, block_rows, 1)
        lifted = jnp.einsum("eaq,qai->aei", hot_rows, mixed_bf, precision=precise)
        level_rows = lax.dynamic_slice_in_dim(alpha_level, offset, block_rows, 1)
        lifted = lifted + level_rows.T[:, :, None] * rows_here[:, None, :]
        targets = lax.dynamic_slice_in_dim(alpha_target, offset, block_rows, 1)
        sigma_out = sigma_out.at[targets.T.reshape(-1)].add(lifted.reshape(-1, NB))
        current = lax.dynamic_slice_in_dim(sigma_out, offset, block_rows, 0)
        sigma_out = lax.dynamic_update_slice_in_dim(sigma_out, current + same_beta, offset, 0)
        return sigma_out, None

    sigma_out, unused = lax.scan(accumulate, jnp.zeros((NA, NB), jnp.float32), jnp.arange(NA // block_rows, dtype=jnp.int32))
    return sigma_out
```

```python
import functools

import jax
import jax.numpy as jnp
from jax import lax
from jax.experimental import pallas as pl
from jax.experimental.pallas import tpu as pltpu
from jax.sharding import PartitionSpec as P

LANES = 128
GROUP = 3
NT = (((1,), (1,)), ((), ()))


def high_low(values):
    high = lax.reduce_precision(values, 8, 7)
    return high, values - high


def local_kernel(
    sizes, me_ref, c_ref, beta_ref, alpha_ref, vt_ref, h_ref, own_ref, *rest
):
    chunks, rows, cols, nexc, blocks = sizes
    out_refs = rest[: blocks - 1]
    density, lifted, weights, same = rest[blocks - 1 :]
    per_tile = LANES // GROUP
    bf16, f32 = jnp.bfloat16, jnp.float32

    def weight_step(t, carry):
        code = alpha_ref[t]
        pair = (code >> 1) & 127
        sign = (2 * (code & 1) - 1).astype(f32)
        q_ids = lax.broadcasted_iota(jnp.int32, (LANES, LANES), 0)
        hot = jnp.where(q_ids == pair, sign, 0.0).astype(bf16)
        u_t = jnp.dot(vt_ref[...], hot, preferred_element_type=f32)
        weights[pl.ds(pl.multiple_of(t * LANES, LANES), LANES), :] = u_t.T
        return carry

    lax.fori_loop(0, rows * nexc // LANES, weight_step, 0)

    groups = beta_ref.shape[0]

    def beta_step(g, carry):
        code = beta_ref[g]
        target = code >> 8
        low = lax.rem(target, cols)
        high = lax.div(target, cols)
        j_ids = lax.broadcasted_iota(jnp.int32, (cols, 2 * LANES), 0)
        hot = jnp.where(j_ids == low, 1.0, 0.0).astype(bf16)
        picked = jnp.dot(c_ref[0], hot, preferred_element_type=f32)
        for k in range(1, chunks):
            picked = jnp.where(
                high == k, jnp.dot(c_ref[k], hot, preferred_element_type=f32), picked
            )
        picked = picked.astype(bf16)
        pair = (code >> 1) & 127
        sign = (2 * (code & 1) - 1).astype(f32)
        lane = lax.broadcasted_iota(jnp.int32, (1, 2 * LANES), 1)
        member = lax.div(lane & (LANES - 1), per_tile)
        slot = pair + LANES * member
        for half in range(2):
            span = slice(half * LANES, (half + 1) * LANES)
            p_ids = lax.broadcasted_iota(jnp.int32, (GROUP * LANES, LANES), 0)
            h_t = jnp.where(p_ids == slot[:, span], sign[:, span], 0.0).astype(bf16)
            d = lax.dot_general(picked[:, span], h_t, NT, preferred_element_type=f32)
            for m in range(GROUP):
                i = (2 * g + half) * GROUP + m
                density[pl.ds(pl.multiple_of(i * rows, rows), rows), :] = d[
                    :, m * LANES : (m + 1) * LANES
                ]
        return carry

    lax.fori_loop(0, groups, beta_step, 0)

    def alpha_step(t, carry):
        parts = []
        for m in range(2):
            a = 2 * t + m
            d = density[pl.ds(a, cols, stride=rows), :].astype(bf16)
            u = weights[pl.ds(pl.multiple_of(a * nexc, 8), nexc), :]
            u = jnp.concatenate([u, h_ref[...]], axis=0).astype(bf16)
            l = lax.dot_general(u, d, NT, preferred_element_type=f32)
            same[pl.ds(a, 1), :] = l[nexc : nexc + 1] + l[nexc + 1 : nexc + 2]
            parts.append(l[:nexc])
        lifted[pl.ds(pl.multiple_of(t * 2 * nexc, 2 * nexc), 2 * nexc), :] = (
            jnp.concatenate(parts, axis=0).astype(bf16)
        )
        return carry

    lax.fori_loop(0, rows // 2, alpha_step, 0)

    me = me_ref[0]
    for s in range(blocks):
        base = (me ^ s) * rows
        total = jnp.zeros((rows, cols), f32)
        for t in range(rows * nexc // LANES // 8):
            hots = []
            for w in range(8):
                target = (alpha_ref[8 * t + w] >> 8) - base
                b_ids = lax.broadcasted_iota(jnp.int32, (rows, LANES), 0)
                hots.append(jnp.where(b_ids == target, 1.0, 0.0).astype(bf16))
            total += jnp.dot(
                jnp.concatenate(hots, axis=1),
                lifted[8 * t * LANES : 8 * (t + 1) * LANES, :],
                preferred_element_type=f32,
            )
        if s == 0:
            own_ref[...] = total + same[...]
        else:
            out_refs[s - 1][...] = total.astype(bf16)


def shards(
    ci_vector,
    one_body,
    pair_integrals,
    beta_target,
    beta_pair,
    beta_sign,
    alpha_target,
    alpha_pair,
    alpha_sign,
):
    rows, cols = ci_vector.shape
    pairs = one_body.shape[0]
    nexc = beta_target.shape[0]
    blocks = lax.axis_size("alpha")
    chunks = lax.axis_size("beta")
    per_tile = LANES // GROUP
    me = lax.axis_index("alpha")
    bf16 = jnp.bfloat16

    civec_bf = ci_vector.astype(bf16)
    gathered = lax.all_gather(civec_bf, "beta", axis=0)

    beta_code = beta_target * 256 + beta_pair * 2 + beta_sign
    own = (lax.axis_index("beta") * cols + jnp.arange(cols, dtype=jnp.int32)) * 256 + 1
    extra = jnp.stack([own + 2 * (pairs + 2), own + 2 * (pairs + 3)])
    beta_code = jnp.concatenate([beta_code, extra]).T
    tiles = -(-cols // (2 * GROUP)) * 2
    beta_code = jnp.pad(beta_code, ((0, tiles * GROUP - cols), (0, 0)))
    beta_code = beta_code.reshape(tiles, GROUP * (nexc + 2))
    beta_code = jnp.pad(beta_code, ((0, 0), (0, LANES - GROUP * (nexc + 2))))
    beta_code = beta_code.reshape(tiles // 2, 1, 2 * LANES)
    alpha_code = (alpha_target * 256 + alpha_pair * 2 + alpha_sign).T
    alpha_code = alpha_code.reshape(rows * nexc // LANES, 1, LANES)

    h_high, h_low = high_low(one_body)
    vt = jnp.zeros((LANES, LANES), bf16)
    vt = vt.at[:pairs, :pairs].set(pair_integrals.T)
    vt = vt.at[pairs + 2, :pairs].set(h_high.astype(bf16))
    vt = vt.at[pairs + 3, :pairs].set(h_low.astype(bf16))
    h_rows = jnp.pad(jnp.stack([h_high, h_low]), ((0, 6), (0, LANES - pairs)))

    sizes = (chunks, rows, cols, nexc, blocks)
    vmem = pl.BlockSpec(memory_space=pltpu.VMEM)
    outs = pl.pallas_call(
        functools.partial(local_kernel, sizes),
        out_shape=[jax.ShapeDtypeStruct((rows, cols), jnp.float32)]
        + [jax.ShapeDtypeStruct((rows, cols), bf16)] * (blocks - 1),
        in_specs=[pl.BlockSpec(memory_space=pltpu.SMEM)] + [vmem] * 5,
        out_specs=[vmem] * blocks,
        scratch_shapes=[
            pltpu.VMEM((tiles * GROUP * rows, LANES), jnp.float32),
            pltpu.VMEM((rows * nexc, cols), bf16),
            pltpu.VMEM((rows * nexc, LANES), jnp.float32),
            pltpu.VMEM((rows, cols), jnp.float32),
        ],
        compiler_params=pltpu.CompilerParams(vmem_limit_bytes=56 * 1024 * 1024),
        name="sigma_local",
    )(me.reshape(1), gathered, beta_code, alpha_code, vt, h_rows)
    total = outs[0]
    for s in range(1, blocks):
        got = lax.ppermute(outs[s], "alpha", [(d, d ^ s) for d in range(blocks)])
        total = total + got.astype(jnp.float32)
    return total


def solution(mesh):
    placed = (
        P("alpha", "beta"),
        P(),
        P(),
        P(None, "beta"),
        P(None, "beta"),
        P(None, "beta"),
        P(None, "alpha"),
        P(None, "alpha"),
        P(None, "alpha"),
    )
    return jax.shard_map(
        shards, mesh=mesh, in_specs=placed, out_specs=P("alpha", "beta"), check_vma=False
    )
```

```python
import functools

import jax
import jax.numpy as jnp
from jax import lax
from jax.experimental import pallas as pl
from jax.experimental.pallas import tpu as pltpu
from jax.sharding import PartitionSpec as P

LANES = 128
UNROLL = 11
GROUP = 3
NT = (((1,), (1,)), ((), ()))


def high_low(values):
    high = lax.reduce_precision(values, 8, 7)
    return high, values - high


def weight_kernel(tiles, alpha_ref, vt_ref, weights_ref):
    for t in range(tiles):
        code = alpha_ref[t]
        pair = (code >> 1) & 127
        sign = (2 * (code & 1) - 1).astype(jnp.float32)
        q_ids = lax.broadcasted_iota(jnp.int32, (LANES, LANES), 0)
        hot = jnp.where(q_ids == pair, sign, 0.0).astype(jnp.bfloat16)
        u_t = jnp.dot(vt_ref[...], hot, preferred_element_type=jnp.float32)
        weights_ref[t * LANES : (t + 1) * LANES, :] = u_t.T.astype(jnp.bfloat16)


def local_kernel(sizes, place_ref, beta_ref, alpha_ref, weights, *rest):
    chunks, rows, cols, nexc, depth, blocks, stride = sizes
    c_refs, rest = rest[:chunks], rest[chunks:]
    own_ref, out_refs, rest = rest[0], rest[1:blocks], rest[blocks:]
    density, lifted, same, picked = rest
    per_tile = LANES // GROUP
    bf16, f32 = jnp.bfloat16, jnp.float32
    groups = beta_ref.shape[0]
    my_alpha, my_beta = place_ref[0], place_ref[1]

    def gather_step(g, carry):
        target = beta_ref[g] >> 8
        low = lax.rem(target, cols)
        high = lax.div(target, cols) ^ my_beta
        j_ids = lax.broadcasted_iota(jnp.int32, (cols, 2 * LANES), 0)
        hot = jnp.where(j_ids == low, 1.0, 0.0).astype(bf16)
        found = jnp.dot(c_refs[0][...], hot, preferred_element_type=f32)
        for k in range(1, chunks):
            found = jnp.where(
                high == k, jnp.dot(c_refs[k][...], hot, preferred_element_type=f32), found
            )
        picked[g] = found.astype(bf16)
        return carry

    lax.fori_loop(0, groups, gather_step, 0, unroll=UNROLL)

    def density_step(g, carry):
        code = beta_ref[g]
        pair = (code >> 1) & 127
        sign = (2 * (code & 1) - 1).astype(f32)
        lane = lax.broadcasted_iota(jnp.int32, (1, 2 * LANES), 1)
        slot = pair + LANES * lax.div(lane & (LANES - 1), per_tile)
        for half in range(2):
            span = slice(half * LANES, (half + 1) * LANES)
            p_ids = lax.broadcasted_iota(jnp.int32, (GROUP * LANES, LANES), 0)
            h_t = jnp.where(p_ids == slot[:, span], sign[:, span], 0.0).astype(bf16)
            d = lax.dot_general(picked[g, :, span], h_t, NT, preferred_element_type=f32)
            for m in range(GROUP):
                i = (2 * g + half) * GROUP + m
                density[pl.ds(pl.multiple_of(i * stride, 8), rows), :] = d[
                    :, m * LANES : (m + 1) * LANES
                ]
        return carry

    lax.fori_loop(0, groups, density_step, 0, unroll=UNROLL)

    def alpha_step(t, carry):
        parts = []
        for m in range(2):
            a = 2 * t + m
            d = density[pl.ds(a, cols, stride=stride), :].astype(bf16)
            u = weights[pl.ds(pl.multiple_of(a * depth, 16), depth), :]
            l = lax.dot_general(u, d, NT, preferred_element_type=f32)
            same[pl.ds(a, 1), :] = l[nexc : nexc + 1] + l[nexc + 1 : nexc + 2]
            parts.append(l[:nexc])
        lifted[pl.ds(pl.multiple_of(t * 2 * nexc, 2 * nexc), 2 * nexc), :] = (
            jnp.concatenate(parts, axis=0).astype(bf16)
        )
        return carry

    lax.fori_loop(0, rows // 2, alpha_step, 0, unroll=8)

    for s in range(blocks):
        base = (my_alpha ^ s) * rows
        total = jnp.zeros((rows, cols), f32)
        for t in range(rows * nexc // LANES // 8):
            hots = []
            for w in range(8):
                target = (alpha_ref[8 * t + w] >> 8) - base
                b_ids = lax.broadcasted_iota(jnp.int32, (rows, LANES), 0)
                hots.append(jnp.where(b_ids == target, 1.0, 0.0).astype(bf16))
            total += jnp.dot(
                jnp.concatenate(hots, axis=1),
                lifted[8 * t * LANES : 8 * (t + 1) * LANES, :],
                preferred_element_type=f32,
            )
        if s == 0:
            own_ref[...] = total + same[...]
        else:
            out_refs[s - 1][...] = total.astype(bf16)


def shards(
    ci_vector,
    one_body,
    pair_integrals,
    beta_target,
    beta_pair,
    beta_sign,
    alpha_target,
    alpha_pair,
    alpha_sign,
):
    rows, cols = ci_vector.shape
    pairs = one_body.shape[0]
    nexc = beta_target.shape[0]
    blocks = lax.axis_size("alpha")
    chunks = lax.axis_size("beta")
    place = jnp.stack([lax.axis_index("alpha"), lax.axis_index("beta")])
    bf16 = jnp.bfloat16

    civec_bf = ci_vector.astype(bf16)
    gathered = [civec_bf] + [
        lax.ppermute(civec_bf, "beta", [(d, d ^ s) for d in range(chunks)])
        for s in range(1, chunks)
    ]

    beta_code = beta_target * 256 + beta_pair * 2 + beta_sign
    own = (lax.axis_index("beta") * cols + jnp.arange(cols, dtype=jnp.int32)) * 256 + 1
    extra = jnp.stack([own + 2 * (pairs + 2), own + 2 * (pairs + 3)])
    beta_code = jnp.concatenate([beta_code, extra]).T
    tiles = -(-cols // (2 * GROUP * UNROLL)) * 2 * UNROLL
    beta_code = jnp.pad(beta_code, ((0, tiles * GROUP - cols), (0, 0)))
    beta_code = beta_code.reshape(tiles, GROUP * (nexc + 2))
    beta_code = jnp.pad(beta_code, ((0, 0), (0, LANES - GROUP * (nexc + 2))))
    beta_code = beta_code.reshape(tiles // 2, 1, 2 * LANES)
    alpha_code = alpha_target * 256 + alpha_pair * 2 + alpha_sign
    depth = nexc + 8
    one_rows = jnp.arange(depth - nexc, dtype=jnp.int32)[:, None] * 2 + 2 * pairs + 1
    one_rows = jnp.broadcast_to(one_rows, (depth - nexc, rows))
    weight_code = jnp.concatenate([alpha_code, one_rows]).T
    weight_code = weight_code.reshape(rows * depth // LANES, 1, LANES)
    alpha_code = alpha_code.T.reshape(rows * nexc // LANES, 1, LANES)

    h_high, h_low = high_low(one_body)
    halves = jnp.stack([h_high, h_low]).astype(bf16)
    corner = jnp.zeros((2, 2), bf16)
    vt = jnp.concatenate(
        [
            jnp.concatenate([pair_integrals.T, halves.T], axis=1),
            jnp.zeros((2, pairs + 2), bf16),
            jnp.concatenate([halves, corner], axis=1),
        ]
    )
    vt = jnp.pad(vt, ((0, LANES - pairs - 4), (0, LANES - pairs - 2)))

    vmem = pl.BlockSpec(memory_space=pltpu.VMEM)
    weights = pl.pallas_call(
        functools.partial(weight_kernel, rows * depth // LANES),
        out_shape=jax.ShapeDtypeStruct((rows * depth, LANES), bf16),
        in_specs=[vmem] * 2,
        out_specs=vmem,
        name="weights",
    )(weight_code, vt)

    stride = rows + 8
    sizes = (chunks, rows, cols, nexc, depth, blocks, stride)
    outs = pl.pallas_call(
        functools.partial(local_kernel, sizes),
        out_shape=[jax.ShapeDtypeStruct((rows, cols), jnp.float32)]
        + [jax.ShapeDtypeStruct((rows, cols), bf16)] * (blocks - 1),
        in_specs=[pl.BlockSpec(memory_space=pltpu.SMEM)] + [vmem] * (3 + chunks),
        out_specs=[vmem] * blocks,
        scratch_shapes=[
            pltpu.VMEM((tiles * GROUP * stride, LANES), jnp.float32),
            pltpu.VMEM((rows * nexc, cols), bf16),
            pltpu.VMEM((rows, cols), jnp.float32),
            pltpu.VMEM((tiles // 2, rows, 2 * LANES), bf16),
        ],
        compiler_params=pltpu.CompilerParams(vmem_limit_bytes=56 * 1024 * 1024),
        name="sigma_local",
    )(place, beta_code, alpha_code, weights, *gathered)
    total = outs[0]
    for s in range(1, blocks):
        got = lax.ppermute(outs[s], "alpha", [(d, d ^ s) for d in range(blocks)])
        total = total + got.astype(jnp.float32)
    return total


def solution(mesh):
    placed = (
        P("alpha", "beta"),
        P(),
        P(),
        P(None, "beta"),
        P(None, "beta"),
        P(None, "beta"),
        P(None, "alpha"),
        P(None, "alpha"),
        P(None, "alpha"),
    )
    return jax.shard_map(
        shards, mesh=mesh, in_specs=placed, out_specs=P("alpha", "beta"), check_vma=False
    )
```

```python
import functools

import jax
import jax.numpy as jnp
from jax import lax
from jax.experimental import pallas as pl
from jax.experimental.pallas import tpu as pltpu
from jax.sharding import PartitionSpec as P

LANES = 128
UNROLL = 11
GROUP = 3
NT = (((1,), (1,)), ((), ()))


def index_kernel(
    sizes,
    own_ref,
    beta_target,
    beta_pair,
    beta_sign,
    alpha_target,
    alpha_pair,
    alpha_sign,
    one_body,
    integrals,
    beta_ref,
    alpha_ref,
    weights_ref,
    table,
    turned,
):
    rows, cols, nexc, depth, tiles, pairs = sizes
    bf16, f32 = jnp.bfloat16, jnp.float32
    per_tile = LANES // GROUP
    lane = lax.broadcasted_iota(jnp.int32, (8, LANES), 1)

    h = one_body[...]
    h_high = h.astype(bf16).astype(f32)
    halves = jnp.concatenate([h_high, h - h_high], axis=0)
    table[...] = jnp.zeros_like(table)
    table[pairs + 2 : pairs + 4, :pairs] = halves
    columns = table[...].T
    table[...] = jnp.zeros_like(table)
    table[:pairs, :pairs] = integrals[...].astype(f32)
    table[pairs : pairs + 2, :pairs] = halves
    rows_of = (table[...] + columns).astype(bf16)

    signed = (2 * alpha_sign[...] - 1) * (alpha_pair[...] + 1)
    after = lax.broadcasted_iota(jnp.int32, (depth - nexc, rows), 0) + pairs + 1
    signed = jnp.concatenate([signed, after], axis=0)
    q_ids = lax.broadcasted_iota(jnp.int32, (depth, LANES), 1) + 1
    batch = 16
    for b in range(rows // batch):
        hots = []
        for a in range(b * batch, (b + 1) * batch):
            column = jnp.broadcast_to(signed[:, a : a + 1], (depth, LANES))
            value = jnp.where(column > 0, 1.0, -1.0)
            hots.append(jnp.where(jnp.abs(column) == q_ids, value, 0.0).astype(bf16))
        u = jnp.dot(jnp.concatenate(hots, axis=0), rows_of, preferred_element_type=f32)
        weights_ref[b * batch * depth : (b + 1) * batch * depth, :] = u.astype(bf16)

    code = beta_target[...] * 256 + beta_pair[...] * 2 + beta_sign[...]
    own = own_ref[0] * cols + lax.broadcasted_iota(jnp.int32, (2, cols), 1)
    extra = lax.broadcasted_iota(jnp.int32, (2, cols), 0) + pairs + 2
    extra = own * 256 + extra * 2 + 1
    blank = jnp.zeros((LANES - nexc - 2, cols), jnp.int32)
    code = jnp.concatenate([code, extra, blank], axis=0).astype(f32)
    turned[...] = jnp.zeros_like(turned)
    for c in range(cols // LANES):
        turned[c * LANES : (c + 1) * LANES, :] = code[:, c * LANES : (c + 1) * LANES].T
    total = jnp.zeros((tiles, LANES), f32)
    for m in range(GROUP):
        part = turned[pl.ds(m, tiles, stride=GROUP), :]
        total += pltpu.roll(part, m * per_tile, 1) if m else part
    total = total.astype(jnp.int32)
    beta_ref[...] = total

    code = jnp.concatenate(
        [alpha_target[...], jnp.zeros((LANES - nexc, rows), jnp.int32)], axis=0
    )
    turned[:rows, :] = code.astype(f32).T
    period = rows * nexc // LANES // 8
    step = period * LANES // nexc
    found = [jnp.zeros((8, LANES), f32) for w in range(period)]
    for j in range(step):
        part = turned[pl.ds(j, 8, stride=step), :]
        w, shift = divmod(j * nexc, LANES)
        part = pltpu.roll(part, shift, 1) if shift else part
        found[w] += jnp.where(lane >= shift, part, 0.0)
        if shift + nexc > LANES:
            found[w + 1] += jnp.where(lane < shift + nexc - LANES, part, 0.0)
    for w in range(period):
        alpha_ref[8 * w : 8 * w + 8, :] = found[w].astype(jnp.int32)


def local_kernel(sizes, place_ref, beta_ref, alpha_ref, weights, *rest):
    chunks, rows, cols, nexc, depth, blocks, stride = sizes
    c_refs, rest = rest[:chunks], rest[chunks:]
    own_ref, out_refs, rest = rest[0], rest[1:blocks], rest[blocks:]
    density, lifted, same, picked = rest
    per_tile = LANES // GROUP
    bf16, f32 = jnp.bfloat16, jnp.float32
    groups = beta_ref.shape[0] // 2
    my_alpha, my_beta = place_ref[0], place_ref[1]

    def beta_code(g):
        return jnp.concatenate([beta_ref[pl.ds(2 * g, 1), :], beta_ref[pl.ds(2 * g + 1, 1), :]], axis=1)

    def gather_step(g, carry):
        target = beta_code(g) >> 8
        low = lax.rem(target, cols)
        high = lax.div(target, cols) ^ my_beta
        j_ids = lax.broadcasted_iota(jnp.int32, (cols, 2 * LANES), 0)
        hot = jnp.where(j_ids == low, 1.0, 0.0).astype(bf16)
        found = jnp.dot(c_refs[0][...], hot, preferred_element_type=f32)
        for k in range(1, chunks):
            found = jnp.where(
                high == k, jnp.dot(c_refs[k][...], hot, preferred_element_type=f32), found
            )
        picked[g] = found.astype(bf16)
        return carry

    lax.fori_loop(0, groups, gather_step, 0, unroll=UNROLL)

    def density_step(g, carry):
        code = beta_code(g)
        pair = (code >> 1) & 127
        sign = (2 * (code & 1) - 1).astype(f32)
        lane = lax.broadcasted_iota(jnp.int32, (1, 2 * LANES), 1)
        slot = pair + LANES * lax.div(lane & (LANES - 1), per_tile)
        for half in range(2):
            span = slice(half * LANES, (half + 1) * LANES)
            p_ids = lax.broadcasted_iota(jnp.int32, (GROUP * LANES, LANES), 0)
            h_t = jnp.where(p_ids == slot[:, span], sign[:, span], 0.0).astype(bf16)
            d = lax.dot_general(picked[g, :, span], h_t, NT, preferred_element_type=f32)
            for m in range(GROUP):
                i = (2 * g + half) * GROUP + m
                density[pl.ds(pl.multiple_of(i * stride, 8), rows), :] = d[
                    :, m * LANES : (m + 1) * LANES
                ]
        return carry

    lax.fori_loop(0, groups, density_step, 0, unroll=UNROLL)

    def alpha_step(t, carry):
        parts = []
        for m in range(2):
            a = 2 * t + m
            d = density[pl.ds(a, cols, stride=stride), :].astype(bf16)
            u = weights[pl.ds(pl.multiple_of(a * depth, 16), depth), :]
            l = lax.dot_general(u, d, NT, preferred_element_type=f32)
            same[pl.ds(a, 1), :] = l[nexc : nexc + 1] + l[nexc + 1 : nexc + 2]
            parts.append(l[:nexc])
        lifted[pl.ds(pl.multiple_of(t * 2 * nexc, 2 * nexc), 2 * nexc), :] = (
            jnp.concatenate(parts, axis=0).astype(bf16)
        )
        return carry

    lax.fori_loop(0, rows // 2, alpha_step, 0, unroll=8)

    for s in range(blocks):
        base = (my_alpha ^ s) * rows
        total = jnp.zeros((rows, cols), f32)
        period = rows * nexc // LANES // 8
        for t in range(8):
            hots = []
            for w in range(period):
                target = alpha_ref[8 * w + t : 8 * w + t + 1, :] - base
                b_ids = lax.broadcasted_iota(jnp.int32, (rows, LANES), 0)
                hots.append(jnp.where(b_ids == target, 1.0, 0.0).astype(bf16))
            total += jnp.dot(
                jnp.concatenate(hots, axis=1),
                lifted[period * t * LANES : period * (t + 1) * LANES, :],
                preferred_element_type=f32,
            )
        if s == 0:
            own_ref[...] = total + same[...]
        else:
            out_refs[s - 1][...] = total.astype(bf16)


def shards(
    ci_vector,
    one_body,
    pair_integrals,
    beta_target,
    beta_pair,
    beta_sign,
    alpha_target,
    alpha_pair,
    alpha_sign,
):
    rows, cols = ci_vector.shape
    pairs = one_body.shape[0]
    nexc = beta_target.shape[0]
    blocks = lax.axis_size("alpha")
    chunks = lax.axis_size("beta")
    place = jnp.stack([lax.axis_index("alpha"), lax.axis_index("beta")])
    bf16 = jnp.bfloat16

    civec_bf = ci_vector.astype(bf16)
    gathered = [civec_bf] + [
        lax.ppermute(civec_bf, "beta", [(d, d ^ s) for d in range(chunks)])
        for s in range(1, chunks)
    ]

    depth = nexc + 8
    tiles = -(-cols // (2 * GROUP * UNROLL)) * 2 * UNROLL
    vmem = pl.BlockSpec(memory_space=pltpu.VMEM)
    beta_code, alpha_code, weights = pl.pallas_call(
        functools.partial(index_kernel, (rows, cols, nexc, depth, tiles, pairs)),
        out_shape=[
            jax.ShapeDtypeStruct((tiles, LANES), jnp.int32),
            jax.ShapeDtypeStruct((rows * nexc // LANES, LANES), jnp.int32),
            jax.ShapeDtypeStruct((rows * depth, LANES), bf16),
        ],
        in_specs=[pl.BlockSpec(memory_space=pltpu.SMEM)] + [vmem] * 8,
        out_specs=[vmem] * 3,
        scratch_shapes=[
            pltpu.VMEM((LANES, LANES), jnp.float32),
            pltpu.VMEM((tiles * GROUP, LANES), jnp.float32),
        ],
        name="index_lists",
    )(
        place[1:],
        beta_target,
        beta_pair,
        beta_sign,
        alpha_target,
        alpha_pair,
        alpha_sign,
        one_body.reshape(1, pairs),
        pair_integrals,
    )

    stride = rows + 8
    sizes = (chunks, rows, cols, nexc, depth, blocks, stride)
    outs = pl.pallas_call(
        functools.partial(local_kernel, sizes),
        out_shape=[jax.ShapeDtypeStruct((rows, cols), jnp.float32)]
        + [jax.ShapeDtypeStruct((rows, cols), bf16)] * (blocks - 1),
        in_specs=[pl.BlockSpec(memory_space=pltpu.SMEM)] + [vmem] * (3 + chunks),
        out_specs=[vmem] * blocks,
        scratch_shapes=[
            pltpu.VMEM((tiles * GROUP * stride, LANES), jnp.float32),
            pltpu.VMEM((rows * nexc, cols), bf16),
            pltpu.VMEM((rows, cols), jnp.float32),
            pltpu.VMEM((tiles // 2, rows, 2 * LANES), bf16),
        ],
        compiler_params=pltpu.CompilerParams(vmem_limit_bytes=56 * 1024 * 1024),
        name="sigma_local",
    )(place, beta_code, alpha_code, weights, *gathered)
    total = outs[0]
    for s in range(1, blocks):
        got = lax.ppermute(outs[s], "alpha", [(d, d ^ s) for d in range(blocks)])
        total = total + got.astype(jnp.float32)
    return total


def solution(mesh):
    placed = (
        P("alpha", "beta"),
        P(),
        P(),
        P(None, "beta"),
        P(None, "beta"),
        P(None, "beta"),
        P(None, "alpha"),
        P(None, "alpha"),
        P(None, "alpha"),
    )
    return jax.shard_map(
        shards, mesh=mesh, in_specs=placed, out_specs=P("alpha", "beta"), check_vma=False
    )
```

```python
import functools

import jax
import jax.numpy as jnp
from jax import lax
from jax.experimental import pallas as pl
from jax.experimental.pallas import tpu as pltpu
from jax.sharding import PartitionSpec as P

LANES = 128
UNROLL = 11
GROUP = 3
NT = (((1,), (1,)), ((), ()))


def index_kernel(
    sizes,
    beta_target,
    beta_pair,
    beta_sign,
    alpha_target,
    alpha_pair,
    alpha_sign,
    one_body,
    integrals,
    beta_ref,
    alpha_ref,
    weights_ref,
    table,
    turned,
):
    rows, cols, nexc, depth, tiles, pairs = sizes
    bf16, f32 = jnp.bfloat16, jnp.float32
    per_tile = LANES // GROUP
    lane = lax.broadcasted_iota(jnp.int32, (8, LANES), 1)

    h = one_body[...]
    h_high = h.astype(bf16).astype(f32)
    halves = jnp.concatenate([h_high, h - h_high], axis=0)
    table[...] = jnp.zeros_like(table)
    table[pairs + 2 : pairs + 4, :pairs] = halves
    columns = table[...].T
    table[...] = jnp.zeros_like(table)
    table[:pairs, :pairs] = integrals[...].astype(f32)
    table[pairs : pairs + 2, :pairs] = halves
    rows_of = (table[...] + columns).astype(bf16)

    signed = (2 * alpha_sign[...] - 1) * (alpha_pair[...] + 1)
    after = lax.broadcasted_iota(jnp.int32, (depth - nexc, rows), 0) + pairs + 1
    signed = jnp.concatenate([signed, after], axis=0)
    q_ids = lax.broadcasted_iota(jnp.int32, (depth, LANES), 1) + 1
    batch = 16
    for b in range(rows // batch):
        hots = []
        for a in range(b * batch, (b + 1) * batch):
            column = jnp.broadcast_to(signed[:, a : a + 1], (depth, LANES))
            value = jnp.where(column > 0, 1.0, -1.0)
            hots.append(jnp.where(jnp.abs(column) == q_ids, value, 0.0).astype(bf16))
        u = jnp.dot(jnp.concatenate(hots, axis=0), rows_of, preferred_element_type=f32)
        weights_ref[b * batch * depth : (b + 1) * batch * depth, :] = u.astype(bf16)

    code = beta_target[...] * 256 + beta_pair[...] * 2 + beta_sign[...]
    own = lax.axis_index("beta") * cols + lax.broadcasted_iota(jnp.int32, (2, cols), 1)
    extra = lax.broadcasted_iota(jnp.int32, (2, cols), 0) + pairs + 2
    extra = own * 256 + extra * 2 + 1
    blank = jnp.zeros((LANES - nexc - 2, cols), jnp.int32)
    code = jnp.concatenate([code, extra, blank], axis=0).astype(f32)
    turned[...] = jnp.zeros_like(turned)
    for c in range(cols // LANES):
        turned[c * LANES : (c + 1) * LANES, :] = code[:, c * LANES : (c + 1) * LANES].T
    total = jnp.zeros((tiles, LANES), f32)
    for m in range(GROUP):
        part = turned[pl.ds(m, tiles, stride=GROUP), :]
        total += pltpu.roll(part, m * per_tile, 1) if m else part
    total = total.astype(jnp.int32)
    beta_ref[...] = total

    code = jnp.concatenate(
        [alpha_target[...], jnp.zeros((LANES - nexc, rows), jnp.int32)], axis=0
    )
    turned[:rows, :] = code.astype(f32).T
    period = rows * nexc // LANES // 8
    step = period * LANES // nexc
    found = [jnp.zeros((8, LANES), f32) for w in range(period)]
    for j in range(step):
        part = turned[pl.ds(j, 8, stride=step), :]
        w, shift = divmod(j * nexc, LANES)
        part = pltpu.roll(part, shift, 1) if shift else part
        found[w] += jnp.where(lane >= shift, part, 0.0)
        if shift + nexc > LANES:
            found[w + 1] += jnp.where(lane < shift + nexc - LANES, part, 0.0)
    for w in range(period):
        alpha_ref[8 * w : 8 * w + 8, :] = found[w].astype(jnp.int32)


def scatter(s, rows, nexc, alpha_ref, lifted):
    base = (lax.axis_index("alpha") ^ s) * rows
    total = jnp.zeros((rows, lifted.shape[1]), jnp.float32)
    period = rows * nexc // LANES // 8
    for t in range(8):
        hots = []
        for w in range(period):
            target = alpha_ref[8 * w + t : 8 * w + t + 1, :] - base
            b_ids = lax.broadcasted_iota(jnp.int32, (rows, LANES), 0)
            hots.append(jnp.where(b_ids == target, 1.0, 0.0).astype(jnp.bfloat16))
        total += jnp.dot(
            jnp.concatenate(hots, axis=1),
            lifted[period * t * LANES : period * (t + 1) * LANES, :],
            preferred_element_type=jnp.float32,
        )
    return total


def far_kernel(sizes, beta_ref, alpha_ref, weights, *rest):
    chunks, rows, cols, nexc, depth, blocks, stride = sizes
    c_refs, rest = rest[:chunks], rest[chunks:]
    lifted, same = rest[:2]
    out_refs, (density, picked) = rest[2:-2], rest[-2:]
    per_tile = LANES // GROUP
    bf16, f32 = jnp.bfloat16, jnp.float32
    groups = beta_ref.shape[0] // 2
    my_beta = lax.axis_index("beta")

    def beta_code(g):
        return jnp.concatenate([beta_ref[pl.ds(2 * g, 1), :], beta_ref[pl.ds(2 * g + 1, 1), :]], axis=1)

    def gather_step(g, carry):
        target = beta_code(g) >> 8
        low = lax.rem(target, cols)
        high = lax.div(target, cols) ^ my_beta
        j_ids = lax.broadcasted_iota(jnp.int32, (cols, 2 * LANES), 0)
        hot = jnp.where(j_ids == low, 1.0, 0.0).astype(bf16)
        found = jnp.dot(c_refs[0][...], hot, preferred_element_type=f32)
        for k in range(1, chunks):
            found = jnp.where(
                high == k, jnp.dot(c_refs[k][...], hot, preferred_element_type=f32), found
            )
        picked[g] = found.astype(bf16)
        return carry

    lax.fori_loop(0, groups, gather_step, 0, unroll=UNROLL)

    def density_step(g, carry):
        code = beta_code(g)
        pair = (code >> 1) & 127
        sign = (2 * (code & 1) - 1).astype(f32)
        lane = lax.broadcasted_iota(jnp.int32, (1, 2 * LANES), 1)
        slot = pair + LANES * lax.div(lane & (LANES - 1), per_tile)
        for half in range(2):
            span = slice(half * LANES, (half + 1) * LANES)
            p_ids = lax.broadcasted_iota(jnp.int32, (GROUP * LANES, LANES), 0)
            h_t = jnp.where(p_ids == slot[:, span], sign[:, span], 0.0).astype(bf16)
            d = lax.dot_general(picked[g, :, span], h_t, NT, preferred_element_type=f32)
            for m in range(GROUP):
                i = (2 * g + half) * GROUP + m
                density[pl.ds(pl.multiple_of(i * stride, 8), rows), :] = d[
                    :, m * LANES : (m + 1) * LANES
                ]
        return carry

    lax.fori_loop(0, groups, density_step, 0, unroll=UNROLL)

    def alpha_step(t, carry):
        parts = []
        for m in range(2):
            a = 2 * t + m
            d = density[pl.ds(a, cols, stride=stride), :].astype(bf16)
            u = weights[pl.ds(pl.multiple_of(a * depth, 16), depth), :]
            l = lax.dot_general(u, d, NT, preferred_element_type=f32)
            same[pl.ds(a, 1), :] = l[nexc : nexc + 1] + l[nexc + 1 : nexc + 2]
            parts.append(l[:nexc])
        lifted[pl.ds(pl.multiple_of(t * 2 * nexc, 2 * nexc), 2 * nexc), :] = (
            jnp.concatenate(parts, axis=0).astype(bf16)
        )
        return carry

    lax.fori_loop(0, rows // 2, alpha_step, 0, unroll=8)

    for s in range(blocks // 2, blocks):
        total = scatter(s, rows, nexc, alpha_ref, lifted)
        out_refs[s - blocks // 2][...] = total.astype(bf16)


def near_kernel(sizes, alpha_ref, lifted, same, own_ref, *out_refs):
    rows, nexc, blocks = sizes
    for s in range(1, blocks // 2):
        total = scatter(s, rows, nexc, alpha_ref, lifted)
        out_refs[s - 1][...] = total.astype(jnp.bfloat16)
    own_ref[...] = scatter(0, rows, nexc, alpha_ref, lifted) + same[...]


def shards(
    ci_vector,
    one_body,
    pair_integrals,
    beta_target,
    beta_pair,
    beta_sign,
    alpha_target,
    alpha_pair,
    alpha_sign,
):
    rows, cols = ci_vector.shape
    pairs = one_body.shape[0]
    nexc = beta_target.shape[0]
    blocks = lax.axis_size("alpha")
    chunks = lax.axis_size("beta")
    bf16 = jnp.bfloat16

    civec_bf = ci_vector.astype(bf16)
    gathered = [civec_bf] + [
        lax.ppermute(civec_bf, "beta", [(d, d ^ s) for d in range(chunks)])
        for s in range(1, chunks)
    ]

    depth = nexc + 8
    tiles = -(-cols // (2 * GROUP * UNROLL)) * 2 * UNROLL
    vmem = pl.BlockSpec(memory_space=pltpu.VMEM)
    beta_code, alpha_code, weights = pl.pallas_call(
        functools.partial(index_kernel, (rows, cols, nexc, depth, tiles, pairs)),
        out_shape=[
            jax.ShapeDtypeStruct((tiles, LANES), jnp.int32),
            jax.ShapeDtypeStruct((rows * nexc // LANES, LANES), jnp.int32),
            jax.ShapeDtypeStruct((rows * depth, LANES), bf16),
        ],
        in_specs=[vmem] * 8,
        out_specs=[vmem] * 3,
        scratch_shapes=[
            pltpu.VMEM((LANES, LANES), jnp.float32),
            pltpu.VMEM((tiles * GROUP, LANES), jnp.float32),
        ],
        cost_estimate=pl.CostEstimate(
            flops=4 * rows * depth * LANES * LANES, bytes_accessed=0, transcendentals=0
        ),
        name="index_lists",
    )(
        beta_target,
        beta_pair,
        beta_sign,
        alpha_target,
        alpha_pair,
        alpha_sign,
        one_body.reshape(1, pairs),
        pair_integrals,
    )

    stride = rows + 8
    sizes = (chunks, rows, cols, nexc, depth, blocks, stride)
    block = jax.ShapeDtypeStruct((rows, cols), bf16)
    block_f32 = jax.ShapeDtypeStruct((rows, cols), jnp.float32)
    lifted, same, *far = pl.pallas_call(
        functools.partial(far_kernel, sizes),
        out_shape=[jax.ShapeDtypeStruct((rows * nexc, cols), bf16), block_f32]
        + [block] * (blocks // 2),
        in_specs=[vmem] * (3 + chunks),
        out_specs=[vmem] * (2 + blocks // 2),
        scratch_shapes=[
            pltpu.VMEM((tiles * GROUP * stride, LANES), jnp.float32),
            pltpu.VMEM((tiles // 2, rows, 2 * LANES), bf16),
        ],
        compiler_params=pltpu.CompilerParams(vmem_limit_bytes=36 * 1024 * 1024),
        name="sigma_far",
    )(beta_code, alpha_code, weights, *gathered)

    def send(s, value):
        return lax.ppermute(value, "alpha", [(d, d ^ s) for d in range(blocks)])

    far_got = [send(blocks // 2 + s, far[s]) for s in range(blocks // 2)]
    own, *near = pl.pallas_call(
        functools.partial(near_kernel, (rows, nexc, blocks)),
        out_shape=[block_f32] + [block] * (blocks // 2 - 1),
        in_specs=[vmem] * 3,
        out_specs=[vmem] * (blocks // 2),
        compiler_params=pltpu.CompilerParams(vmem_limit_bytes=8 * 1024 * 1024),
        cost_estimate=pl.CostEstimate(
            flops=blocks * rows * rows * nexc * cols, bytes_accessed=0, transcendentals=0
        ),
        name="sigma_near",
    )(alpha_code, lifted, same)
    *near, far_got[0] = lax.optimization_barrier((*near, far_got[0]))
    total = own
    for got in [send(s + 1, near[s]) for s in range(blocks // 2 - 1)] + far_got:
        total = total + got.astype(jnp.float32)
    return total


def solution(mesh):
    placed = (
        P("alpha", "beta"),
        P(),
        P(),
        P(None, "beta"),
        P(None, "beta"),
        P(None, "beta"),
        P(None, "alpha"),
        P(None, "alpha"),
        P(None, "alpha"),
    )
    return jax.shard_map(
        shards, mesh=mesh, in_specs=placed, out_specs=P("alpha", "beta"), check_vma=False
    )
```

```python
import functools

import jax
import jax.numpy as jnp
from jax import lax
from jax.experimental import pallas as pl
from jax.experimental.pallas import tpu as pltpu
from jax.sharding import PartitionSpec as P

LANES = 128
UNROLL = 11
GROUP = 3
NT = (((1,), (1,)), ((), ()))


def index_kernel(sizes, *refs):
    rows, cols, nexc, depth, tiles, pairs = sizes
    sources, (beta_ref, alpha_ref, weights_ref) = refs[:8], refs[8:11]
    staged, (table, turned, arrived) = refs[11:19], refs[19:]
    copies = [
        pltpu.make_async_copy(source, target, arrived.at[n])
        for n, (source, target) in enumerate(zip(sources, staged))
    ]
    for copy in copies:
        copy.start()
    for copy in copies:
        copy.wait()
    beta_target, beta_pair, beta_sign, alpha_target, alpha_pair, alpha_sign = staged[:6]
    one_body, integrals = staged[6:]
    bf16, f32 = jnp.bfloat16, jnp.float32
    per_tile = LANES // GROUP
    lane = lax.broadcasted_iota(jnp.int32, (8, LANES), 1)

    h = one_body[...]
    h_high = h.astype(bf16).astype(f32)
    halves = jnp.concatenate([h_high, h - h_high], axis=0)
    table[...] = jnp.zeros_like(table)
    table[pairs + 2 : pairs + 4, :pairs] = halves
    columns = table[...].T
    table[...] = jnp.zeros_like(table)
    table[:pairs, :pairs] = integrals[...].astype(f32)
    table[pairs : pairs + 2, :pairs] = halves
    rows_of = (table[...] + columns).astype(bf16)

    signed = (2 * alpha_sign[...] - 1) * (alpha_pair[...] + 1)
    after = lax.broadcasted_iota(jnp.int32, (depth - nexc, rows), 0) + pairs + 1
    signed = jnp.concatenate([signed, after], axis=0)
    q_ids = lax.broadcasted_iota(jnp.int32, (depth, LANES), 1) + 1
    batch = 16
    for b in range(rows // batch):
        hots = []
        for a in range(b * batch, (b + 1) * batch):
            column = jnp.broadcast_to(signed[:, a : a + 1], (depth, LANES))
            value = jnp.where(column > 0, 1.0, -1.0)
            hots.append(jnp.where(jnp.abs(column) == q_ids, value, 0.0).astype(bf16))
        u = jnp.dot(jnp.concatenate(hots, axis=0), rows_of, preferred_element_type=f32)
        weights_ref[b * batch * depth : (b + 1) * batch * depth, :] = u.astype(bf16)

    code = beta_target[...] * 256 + beta_pair[...] * 2 + beta_sign[...]
    own = lax.axis_index("beta") * cols + lax.broadcasted_iota(jnp.int32, (2, cols), 1)
    extra = lax.broadcasted_iota(jnp.int32, (2, cols), 0) + pairs + 2
    extra = own * 256 + extra * 2 + 1
    blank = jnp.zeros((LANES - nexc - 2, cols), jnp.int32)
    code = jnp.concatenate([code, extra, blank], axis=0).astype(f32)
    turned[...] = jnp.zeros_like(turned)
    for c in range(cols // LANES):
        turned[c * LANES : (c + 1) * LANES, :] = code[:, c * LANES : (c + 1) * LANES].T
    total = jnp.zeros((tiles, LANES), f32)
    for m in range(GROUP):
        part = turned[pl.ds(m, tiles, stride=GROUP), :]
        total += pltpu.roll(part, m * per_tile, 1) if m else part
    total = total.astype(jnp.int32)
    beta_ref[...] = total

    code = jnp.concatenate(
        [alpha_target[...], jnp.zeros((LANES - nexc, rows), jnp.int32)], axis=0
    )
    turned[:rows, :] = code.astype(f32).T
    period = rows * nexc // LANES // 8
    step = period * LANES // nexc
    found = [jnp.zeros((8, LANES), f32) for w in range(period)]
    for j in range(step):
        part = turned[pl.ds(j, 8, stride=step), :]
        w, shift = divmod(j * nexc, LANES)
        part = pltpu.roll(part, shift, 1) if shift else part
        found[w] += jnp.where(lane >= shift, part, 0.0)
        if shift + nexc > LANES:
            found[w + 1] += jnp.where(lane < shift + nexc - LANES, part, 0.0)
    for w in range(period):
        alpha_ref[8 * w : 8 * w + 8, :] = found[w].astype(jnp.int32)


def scatter(s, rows, nexc, alpha_ref, lifted):
    base = (lax.axis_index("alpha") ^ s) * rows
    total = jnp.zeros((rows, lifted.shape[1]), jnp.float32)
    period = rows * nexc // LANES // 8
    for t in range(8):
        hots = []
        for w in range(period):
            target = alpha_ref[8 * w + t : 8 * w + t + 1, :] - base
            b_ids = lax.broadcasted_iota(jnp.int32, (rows, LANES), 0)
            hots.append(jnp.where(b_ids == target, 1.0, 0.0).astype(jnp.bfloat16))
        total += jnp.dot(
            jnp.concatenate(hots, axis=1),
            lifted[period * t * LANES : period * (t + 1) * LANES, :],
            preferred_element_type=jnp.float32,
        )
    return total


def far_kernel(sizes, beta_ref, alpha_ref, weights, *rest):
    chunks, rows, cols, nexc, depth, blocks, stride = sizes
    c_refs, rest = rest[:chunks], rest[chunks:]
    lifted, same = rest[:2]
    out_refs, (density, picked) = rest[2:-2], rest[-2:]
    per_tile = LANES // GROUP
    bf16, f32 = jnp.bfloat16, jnp.float32
    groups = beta_ref.shape[0] // 2
    my_beta = lax.axis_index("beta")

    def beta_code(g):
        return jnp.concatenate([beta_ref[pl.ds(2 * g, 1), :], beta_ref[pl.ds(2 * g + 1, 1), :]], axis=1)

    def gather_step(g, carry):
        target = beta_code(g) >> 8
        low = lax.rem(target, cols)
        high = lax.div(target, cols) ^ my_beta
        j_ids = lax.broadcasted_iota(jnp.int32, (cols, 2 * LANES), 0)
        hot = jnp.where(j_ids == low, 1.0, 0.0).astype(bf16)
        found = jnp.dot(c_refs[0][...], hot, preferred_element_type=f32)
        for k in range(1, chunks):
            found = jnp.where(
                high == k, jnp.dot(c_refs[k][...], hot, preferred_element_type=f32), found
            )
        picked[g] = found.astype(bf16)
        return carry

    lax.fori_loop(0, groups, gather_step, 0, unroll=UNROLL)

    def density_step(g, carry):
        code = beta_code(g)
        pair = (code >> 1) & 127
        sign = (2 * (code & 1) - 1).astype(f32)
        lane = lax.broadcasted_iota(jnp.int32, (1, 2 * LANES), 1)
        slot = pair + LANES * lax.div(lane & (LANES - 1), per_tile)
        for half in range(2):
            span = slice(half * LANES, (half + 1) * LANES)
            p_ids = lax.broadcasted_iota(jnp.int32, (GROUP * LANES, LANES), 0)
            h_t = jnp.where(p_ids == slot[:, span], sign[:, span], 0.0).astype(bf16)
            d = lax.dot_general(picked[g, :, span], h_t, NT, preferred_element_type=f32)
            for m in range(GROUP):
                i = (2 * g + half) * GROUP + m
                density[pl.ds(pl.multiple_of(i * stride, 8), rows), :] = d[
                    :, m * LANES : (m + 1) * LANES
                ]
        return carry

    lax.fori_loop(0, groups, density_step, 0, unroll=UNROLL)

    def alpha_step(t, carry):
        parts = []
        for m in range(2):
            a = 2 * t + m
            d = density[pl.ds(a, cols, stride=stride), :].astype(bf16)
            u = weights[pl.ds(pl.multiple_of(a * depth, 16), depth), :]
            l = lax.dot_general(u, d, NT, preferred_element_type=f32)
            same[pl.ds(a, 1), :] = l[nexc : nexc + 1] + l[nexc + 1 : nexc + 2]
            parts.append(l[:nexc])
        lifted[pl.ds(pl.multiple_of(t * 2 * nexc, 2 * nexc), 2 * nexc), :] = (
            jnp.concatenate(parts, axis=0).astype(bf16)
        )
        return carry

    lax.fori_loop(0, rows // 2, alpha_step, 0, unroll=8)

    for s in range(blocks // 2, blocks):
        total = scatter(s, rows, nexc, alpha_ref, lifted)
        out_refs[s - blocks // 2][...] = total.astype(bf16)


def near_kernel(sizes, alpha_ref, lifted, same, own_ref, *out_refs):
    rows, nexc, blocks = sizes
    for s in range(1, blocks // 2):
        total = scatter(s, rows, nexc, alpha_ref, lifted)
        out_refs[s - 1][...] = total.astype(jnp.bfloat16)
    own_ref[...] = scatter(0, rows, nexc, alpha_ref, lifted) + same[...]


def shards(
    ci_vector,
    one_body,
    pair_integrals,
    beta_target,
    beta_pair,
    beta_sign,
    alpha_target,
    alpha_pair,
    alpha_sign,
):
    rows, cols = ci_vector.shape
    pairs = one_body.shape[0]
    nexc = beta_target.shape[0]
    blocks = lax.axis_size("alpha")
    chunks = lax.axis_size("beta")
    bf16 = jnp.bfloat16

    civec_bf = ci_vector.astype(bf16)
    gathered = [civec_bf] + [
        lax.ppermute(civec_bf, "beta", [(d, d ^ s) for d in range(chunks)])
        for s in range(1, chunks)
    ]

    depth = nexc + 8
    tiles = -(-cols // (2 * GROUP * UNROLL)) * 2 * UNROLL
    vmem = pl.BlockSpec(memory_space=pltpu.VMEM)
    lists = (
        beta_target,
        beta_pair,
        beta_sign,
        alpha_target,
        alpha_pair,
        alpha_sign,
        one_body.reshape(1, pairs),
        pair_integrals,
    )
    beta_code, alpha_code, weights = pl.pallas_call(
        functools.partial(index_kernel, (rows, cols, nexc, depth, tiles, pairs)),
        out_shape=[
            pltpu.VMEM((tiles, LANES), jnp.int32),
            pltpu.VMEM((rows * nexc // LANES, LANES), jnp.int32),
            pltpu.VMEM((rows * depth, LANES), bf16),
        ],
        in_specs=[pl.BlockSpec(memory_space=pltpu.HBM)] * 8,
        out_specs=[vmem] * 3,
        scratch_shapes=[pltpu.VMEM(x.shape, x.dtype) for x in lists]
        + [
            pltpu.VMEM((LANES, LANES), jnp.float32),
            pltpu.VMEM((tiles * GROUP, LANES), jnp.float32),
            pltpu.SemaphoreType.DMA((len(lists),)),
        ],
        cost_estimate=pl.CostEstimate(
            flops=4 * rows * depth * LANES * LANES, bytes_accessed=0, transcendentals=0
        ),
        compiler_params=pltpu.CompilerParams(vmem_limit_bytes=16 * 1024 * 1024),
        name="index_lists",
    )(*[pltpu.with_memory_space_constraint(x, pltpu.HBM) for x in lists])

    stride = rows + 8
    sizes = (chunks, rows, cols, nexc, depth, blocks, stride)
    block = jax.ShapeDtypeStruct((rows, cols), bf16)
    block_f32 = jax.ShapeDtypeStruct((rows, cols), jnp.float32)
    lifted, same, *far = pl.pallas_call(
        functools.partial(far_kernel, sizes),
        out_shape=[jax.ShapeDtypeStruct((rows * nexc, cols), bf16), block_f32]
        + [block] * (blocks // 2),
        in_specs=[vmem] * (3 + chunks),
        out_specs=[vmem] * (2 + blocks // 2),
        scratch_shapes=[
            pltpu.VMEM((tiles * GROUP * stride, LANES), jnp.float32),
            pltpu.VMEM((tiles // 2, rows, 2 * LANES), bf16),
        ],
        compiler_params=pltpu.CompilerParams(vmem_limit_bytes=36 * 1024 * 1024),
        name="sigma_far",
    )(beta_code, alpha_code, weights, *gathered)

    def send(s, value):
        return lax.ppermute(value, "alpha", [(d, d ^ s) for d in range(blocks)])

    far_sum = far[0].astype(jnp.float32)
    for s in range(1, blocks // 2):
        far_sum = far_sum + send(s, far[s]).astype(jnp.float32)
    far_sum = far_sum.astype(bf16)
    own, *near = pl.pallas_call(
        functools.partial(near_kernel, (rows, nexc, blocks)),
        out_shape=[block_f32] + [block] * (blocks // 2 - 1),
        in_specs=[vmem] * 3,
        out_specs=[vmem] * (blocks // 2),
        compiler_params=pltpu.CompilerParams(vmem_limit_bytes=8 * 1024 * 1024),
        cost_estimate=pl.CostEstimate(
            flops=blocks * rows * rows * nexc * cols, bytes_accessed=0, transcendentals=0
        ),
        name="sigma_near",
    )(alpha_code, lifted, same)
    crossing = send(blocks // 2, far_sum)
    total = own
    for got in [send(s + 1, near[s]) for s in range(blocks // 2 - 1)] + [crossing]:
        total = total + got.astype(jnp.float32)
    return total


def solution(mesh):
    placed = (
        P("alpha", "beta"),
        P(),
        P(),
        P(None, "beta"),
        P(None, "beta"),
        P(None, "beta"),
        P(None, "alpha"),
        P(None, "alpha"),
        P(None, "alpha"),
    )
    return jax.shard_map(
        shards, mesh=mesh, in_specs=placed, out_specs=P("alpha", "beta"), check_vma=False
    )
```

```python
import functools

import jax
import jax.numpy as jnp
from jax import lax
from jax.experimental import pallas as pl
from jax.experimental.pallas import tpu as pltpu
from jax.sharding import PartitionSpec as P

LANES = 128
EARLY = 2
GROUP = 3
NT = (((1,), (1,)), ((), ()))


def index_kernel(sizes, *refs):
    rows, cols, nexc, depth, tiles, pairs = sizes
    sources, (beta_ref, slot_ref, alpha_ref, weights_ref) = refs[:8], refs[8:12]
    staged, (table, turned, arrived) = refs[12:20], refs[20:]
    copies = [
        pltpu.make_async_copy(source, target, arrived.at[n])
        for n, (source, target) in enumerate(zip(sources, staged))
    ]
    for copy in copies:
        copy.start()
    for copy in copies:
        copy.wait()
    beta_target, beta_pair, beta_sign, alpha_target, alpha_pair, alpha_sign = staged[:6]
    one_body, integrals = staged[6:]
    bf16, f32 = jnp.bfloat16, jnp.float32
    per_tile = LANES // GROUP
    lane = lax.broadcasted_iota(jnp.int32, (8, LANES), 1)

    h = one_body[...]
    h_high = h.astype(bf16).astype(f32)
    halves = jnp.concatenate([h_high, h - h_high], axis=0)
    table[...] = jnp.zeros_like(table)
    table[pairs + 2 : pairs + 4, :pairs] = halves
    columns = table[...].T
    table[...] = jnp.zeros_like(table)
    table[:pairs, :pairs] = integrals[...].astype(f32)
    table[pairs : pairs + 2, :pairs] = halves
    rows_of = (table[...] + columns).astype(bf16)

    signed = (2 * alpha_sign[...] - 1) * (alpha_pair[...] + 1)
    after = lax.broadcasted_iota(jnp.int32, (depth - nexc, rows), 0) + pairs + 1
    signed = jnp.concatenate([signed, after], axis=0)
    q_ids = lax.broadcasted_iota(jnp.int32, (depth, LANES), 1) + 1
    batch = 16
    for b in range(rows // batch):
        hots = []
        for a in range(b * batch, (b + 1) * batch):
            column = jnp.broadcast_to(signed[:, a : a + 1], (depth, LANES))
            value = jnp.where(column > 0, 1.0, -1.0)
            hots.append(jnp.where(jnp.abs(column) == q_ids, value, 0.0).astype(bf16))
        u = jnp.dot(jnp.concatenate(hots, axis=0), rows_of, preferred_element_type=f32)
        weights_ref[b * batch * depth : (b + 1) * batch * depth, :] = u.astype(bf16)

    code = beta_target[...] * 256 + beta_pair[...] * 2 + beta_sign[...]
    own = lax.axis_index("beta") * cols + lax.broadcasted_iota(jnp.int32, (2, cols), 1)
    extra = lax.broadcasted_iota(jnp.int32, (2, cols), 0) + pairs + 2
    extra = own * 256 + extra * 2 + 1
    blank = jnp.zeros((LANES - nexc - 2, cols), jnp.int32)
    code = jnp.concatenate([code, extra, blank], axis=0).astype(f32)
    turned[...] = jnp.zeros_like(turned)
    for c in range(cols // LANES):
        turned[c * LANES : (c + 1) * LANES, :] = code[:, c * LANES : (c + 1) * LANES].T
    total = jnp.zeros((tiles, LANES), f32)
    for m in range(GROUP):
        part = turned[pl.ds(m, tiles, stride=GROUP), :]
        total += pltpu.roll(part, m * per_tile, 1) if m else part
    total = total.astype(jnp.int32)
    beta_ref[...] = total
    member = lax.div(lax.broadcasted_iota(jnp.int32, (tiles, LANES), 1), per_tile)
    slot = ((total >> 1) & 127) + LANES * member + 1
    slot = jnp.where((total & 1) == 1, slot, -slot).astype(f32)
    turned[:LANES, :] = jnp.zeros((LANES, LANES), f32)
    turned[:tiles, :] = slot
    slot_ref[...] = turned[:LANES, :].T.astype(jnp.int32)

    code = jnp.concatenate(
        [alpha_target[...], jnp.zeros((LANES - nexc, rows), jnp.int32)], axis=0
    )
    turned[:rows, :] = code.astype(f32).T
    period = rows * nexc // LANES // 8
    step = period * LANES // nexc
    found = [jnp.zeros((8, LANES), f32) for w in range(period)]
    for j in range(step):
        part = turned[pl.ds(j, 8, stride=step), :]
        w, shift = divmod(j * nexc, LANES)
        part = pltpu.roll(part, shift, 1) if shift else part
        found[w] += jnp.where(lane >= shift, part, 0.0)
        if shift + nexc > LANES:
            found[w + 1] += jnp.where(lane < shift + nexc - LANES, part, 0.0)
    for w in range(period):
        alpha_ref[8 * w : 8 * w + 8, :] = found[w].astype(jnp.int32)


def scatter(s, rows, nexc, alpha_ref, lifted):
    base = (lax.axis_index("alpha") ^ s) * rows
    total = jnp.zeros((rows, lifted.shape[1]), jnp.float32)
    period = rows * nexc // LANES // 8
    for t in range(8):
        hots = []
        for w in range(period):
            target = alpha_ref[8 * w + t : 8 * w + t + 1, :] - base
            b_ids = lax.broadcasted_iota(jnp.int32, (rows, LANES), 0)
            hots.append(jnp.where(b_ids == target, 1.0, 0.0).astype(jnp.bfloat16))
        total += jnp.dot(
            jnp.concatenate(hots, axis=1),
            lifted[period * t * LANES : period * (t + 1) * LANES, :],
            preferred_element_type=jnp.float32,
        )
    return total


def pick(g, cols, beta_ref, c_refs, first, found):
    code = jnp.concatenate([beta_ref[2 * g : 2 * g + 1], beta_ref[2 * g + 1 : 2 * g + 2]], axis=1)
    target = code >> 8
    low = lax.rem(target, cols)
    high = lax.div(target, cols) ^ lax.axis_index("beta")
    j_ids = lax.broadcasted_iota(jnp.int32, (cols, 2 * LANES), 0)
    hot = jnp.where(j_ids == low, 1.0, 0.0).astype(jnp.bfloat16)
    for k, c_ref in enumerate(c_refs):
        here = jnp.dot(c_ref[...], hot, preferred_element_type=jnp.float32)
        found = here if found is None else jnp.where(high == first + k, here, found)
    return found


def early_kernel(cols, beta_ref, *rest):
    c_refs, early_ref = rest[:-1], rest[-1]
    for g in range(early_ref.shape[0]):
        early_ref[g] = pick(g, cols, beta_ref, c_refs, 0, None)


def far_kernel(sizes, beta_ref, slot_ref, alpha_ref, weights, early_ref, *rest):
    chunks, rows, cols, nexc, depth, blocks, stride = sizes
    c_refs, rest = rest[: chunks - EARLY], rest[chunks - EARLY :]
    lifted, same = rest[:2]
    out_refs, (density, picked) = rest[2:-2], rest[-2:]
    per_tile = LANES // GROUP
    bf16, f32 = jnp.bfloat16, jnp.float32
    groups = early_ref.shape[0]

    for g in range(groups):
        found = pick(g, cols, beta_ref, c_refs, EARLY, early_ref[g])
        picked[g] = found.astype(bf16)

    ids = lax.broadcasted_iota(jnp.int32, (LANES, LANES), 1) + 1
    for t in range(2 * groups):
        slot = jnp.broadcast_to(slot_ref[:, t : t + 1], (LANES, LANES))
        value = jnp.where(slot > 0, 1.0, -1.0)
        slot = jnp.abs(slot)
        hots = []
        for m in range(GROUP):
            low = m * per_tile // 16 * 16
            high = min(-(-(m + 1) * per_tile // 16) * 16, LANES)
            part = slot[low:high] == ids[low:high] + m * LANES
            part = [jnp.where(part, value[low:high], 0.0).astype(bf16)]
            if low:
                part.insert(0, jnp.zeros((low, LANES), bf16))
            if high < LANES:
                part.append(jnp.zeros((LANES - high, LANES), bf16))
            hots.append(jnp.concatenate(part, axis=0))
        span = slice(t % 2 * LANES, (t % 2 + 1) * LANES)
        d = jnp.dot(
            picked[t // 2, :, span],
            jnp.concatenate(hots, axis=1),
            preferred_element_type=f32,
        )
        for m in range(GROUP):
            i = t * GROUP + m
            density[i * stride : i * stride + rows, :] = d[:, m * LANES : (m + 1) * LANES]

    def alpha_step(t, carry):
        parts = []
        for m in range(2):
            a = 2 * t + m
            d = density[pl.ds(a, cols, stride=stride), :].astype(bf16)
            u = weights[pl.ds(pl.multiple_of(a * depth, 16), depth), :]
            l = lax.dot_general(u, d, NT, preferred_element_type=f32)
            same[pl.ds(a, 1), :] = l[nexc : nexc + 1] + l[nexc + 1 : nexc + 2]
            parts.append(l[:nexc])
        lifted[pl.ds(pl.multiple_of(t * 2 * nexc, 2 * nexc), 2 * nexc), :] = (
            jnp.concatenate(parts, axis=0).astype(bf16)
        )
        return carry

    lax.fori_loop(0, rows // 2, alpha_step, 0, unroll=32)

    for s in range(blocks // 2, blocks):
        total = scatter(s, rows, nexc, alpha_ref, lifted)
        out_refs[s - blocks // 2][...] = total.astype(bf16)


def near_kernel(sizes, alpha_ref, lifted, same, own_ref, *out_refs):
    rows, nexc, blocks = sizes
    for s in range(1, blocks // 2):
        total = scatter(s, rows, nexc, alpha_ref, lifted)
        out_refs[s - 1][...] = total.astype(jnp.bfloat16)
    own_ref[...] = scatter(0, rows, nexc, alpha_ref, lifted) + same[...]


def shards(
    ci_vector,
    one_body,
    pair_integrals,
    beta_target,
    beta_pair,
    beta_sign,
    alpha_target,
    alpha_pair,
    alpha_sign,
):
    rows, cols = ci_vector.shape
    pairs = one_body.shape[0]
    nexc = beta_target.shape[0]
    blocks = lax.axis_size("alpha")
    chunks = lax.axis_size("beta")
    bf16 = jnp.bfloat16

    civec_bf = ci_vector.astype(bf16)
    gathered = [civec_bf] + [
        lax.ppermute(civec_bf, "beta", [(d, d ^ s) for d in range(chunks)])
        for s in range(1, chunks)
    ]

    depth = nexc + 8
    tiles = -(-cols // (2 * GROUP)) * 2
    vmem = pl.BlockSpec(memory_space=pltpu.VMEM)
    lists = (
        beta_target,
        beta_pair,
        beta_sign,
        alpha_target,
        alpha_pair,
        alpha_sign,
        one_body.reshape(1, pairs),
        pair_integrals,
    )
    beta_code, beta_slot, alpha_code, weights = pl.pallas_call(
        functools.partial(index_kernel, (rows, cols, nexc, depth, tiles, pairs)),
        out_shape=[
            pltpu.VMEM((tiles, LANES), jnp.int32),
            pltpu.VMEM((LANES, LANES), jnp.int32),
            pltpu.VMEM((rows * nexc // LANES, LANES), jnp.int32),
            pltpu.VMEM((rows * depth, LANES), bf16),
        ],
        in_specs=[pl.BlockSpec(memory_space=pltpu.HBM)] * 8,
        out_specs=[vmem] * 4,
        scratch_shapes=[pltpu.VMEM(x.shape, x.dtype) for x in lists]
        + [
            pltpu.VMEM((LANES, LANES), jnp.float32),
            pltpu.VMEM((tiles * GROUP, LANES), jnp.float32),
            pltpu.SemaphoreType.DMA((len(lists),)),
        ],
        cost_estimate=pl.CostEstimate(
            flops=4 * rows * depth * LANES * LANES, bytes_accessed=0, transcendentals=0
        ),
        compiler_params=pltpu.CompilerParams(vmem_limit_bytes=16 * 1024 * 1024),
        name="index_lists",
    )(*[pltpu.with_memory_space_constraint(x, pltpu.HBM) for x in lists])

    stride = rows + 8
    early = pl.pallas_call(
        functools.partial(early_kernel, cols),
        out_shape=pltpu.VMEM((tiles // 2, rows, 2 * LANES), jnp.float32),
        in_specs=[vmem] * (1 + EARLY),
        out_specs=vmem,
        compiler_params=pltpu.CompilerParams(vmem_limit_bytes=12 * 1024 * 1024),
        cost_estimate=pl.CostEstimate(
            flops=4 * rows * cols * tiles * LANES, bytes_accessed=0, transcendentals=0
        ),
        name="gather_early",
    )(beta_code, *gathered[:EARLY])
    sizes = (chunks, rows, cols, nexc, depth, blocks, stride)
    block = jax.ShapeDtypeStruct((rows, cols), bf16)
    block_f32 = jax.ShapeDtypeStruct((rows, cols), jnp.float32)
    lifted, same, *far = pl.pallas_call(
        functools.partial(far_kernel, sizes),
        out_shape=[jax.ShapeDtypeStruct((rows * nexc, cols), bf16), block_f32]
        + [block] * (blocks // 2),
        in_specs=[vmem] * (5 + chunks - EARLY),
        out_specs=[vmem] * (2 + blocks // 2),
        scratch_shapes=[
            pltpu.VMEM((tiles * GROUP * stride, LANES), jnp.float32),
            pltpu.VMEM((tiles // 2, rows, 2 * LANES), bf16),
        ],
        compiler_params=pltpu.CompilerParams(vmem_limit_bytes=36 * 1024 * 1024),
        name="sigma_far",
    )(beta_code, beta_slot, alpha_code, weights, early, *gathered[EARLY:])

    def send(s, value):
        return lax.ppermute(value, "alpha", [(d, d ^ s) for d in range(blocks)])

    far_sum = far[0].astype(jnp.float32)
    for s in range(1, blocks // 2):
        far_sum = far_sum + send(s, far[s]).astype(jnp.float32)
    far_sum = far_sum.astype(bf16)
    own, *near = pl.pallas_call(
        functools.partial(near_kernel, (rows, nexc, blocks)),
        out_shape=[block_f32] + [block] * (blocks // 2 - 1),
        in_specs=[vmem] * 3,
        out_specs=[vmem] * (blocks // 2),
        compiler_params=pltpu.CompilerParams(vmem_limit_bytes=8 * 1024 * 1024),
        cost_estimate=pl.CostEstimate(
            flops=blocks * rows * rows * nexc * cols, bytes_accessed=0, transcendentals=0
        ),
        name="sigma_near",
    )(alpha_code, lifted, same)
    crossing = send(blocks // 2, far_sum)
    total = own
    for got in [send(s + 1, near[s]) for s in range(blocks // 2 - 1)] + [crossing]:
        total = total + got.astype(jnp.float32)
    return total


def solution(mesh):
    placed = (
        P("alpha", "beta"),
        P(),
        P(),
        P(None, "beta"),
        P(None, "beta"),
        P(None, "beta"),
        P(None, "alpha"),
        P(None, "alpha"),
        P(None, "alpha"),
    )
    return jax.shard_map(
        shards, mesh=mesh, in_specs=placed, out_specs=P("alpha", "beta"), check_vma=False
    )
```

```python
import functools

import jax
import jax.numpy as jnp
from jax import lax
from jax.experimental import pallas as pl
from jax.experimental.pallas import tpu as pltpu
from jax.sharding import PartitionSpec as P

LANES = 128
BATCH = 32
EARLY = 2
GROUP = 3
NT = (((1,), (1,)), ((), ()))


def index_kernel(sizes, *refs):
    rows, cols, nexc, depth, tiles, pairs = sizes
    sources, (beta_ref, slot_ref, alpha_ref, weights_ref) = refs[:8], refs[8:12]
    staged, (table, turned, arrived) = refs[12:20], refs[20:]
    copies = [
        pltpu.make_async_copy(source, target, arrived.at[n])
        for n, (source, target) in enumerate(zip(sources, staged))
    ]
    for copy in copies:
        copy.start()
    for copy in copies:
        copy.wait()
    beta_target, beta_pair, beta_sign, alpha_target, alpha_pair, alpha_sign = staged[:6]
    one_body, integrals = staged[6:]
    bf16, f32 = jnp.bfloat16, jnp.float32
    per_tile = LANES // GROUP
    lane = lax.broadcasted_iota(jnp.int32, (8, LANES), 1)

    h = one_body[...]
    h_high = h.astype(bf16).astype(f32)
    halves = jnp.concatenate([h_high, h - h_high], axis=0)
    table[...] = jnp.zeros_like(table)
    table[pairs + 2 : pairs + 4, :pairs] = halves
    columns = table[...].T
    table[...] = jnp.zeros_like(table)
    table[:pairs, :pairs] = integrals[...].astype(f32)
    table[pairs : pairs + 2, :pairs] = halves
    rows_of = (table[...] + columns).astype(bf16)

    signed = (2 * alpha_sign[...] - 1) * (alpha_pair[...] + 1)
    after = lax.broadcasted_iota(jnp.int32, (depth - nexc, rows), 0) + pairs + 1
    signed = jnp.concatenate([signed, after], axis=0)
    q_ids = lax.broadcasted_iota(jnp.int32, (depth, LANES), 1) + 1
    batch = 16
    for b in range(rows // batch):
        hots = []
        for a in range(b * batch, (b + 1) * batch):
            column = jnp.broadcast_to(signed[:, a : a + 1], (depth, LANES))
            value = jnp.where(column > 0, 1.0, -1.0)
            hots.append(jnp.where(jnp.abs(column) == q_ids, value, 0.0).astype(bf16))
        u = jnp.dot(jnp.concatenate(hots, axis=0), rows_of, preferred_element_type=f32)
        weights_ref[b * batch * depth : (b + 1) * batch * depth, :] = u.astype(bf16)

    code = beta_target[...] * 256 + beta_pair[...] * 2 + beta_sign[...]
    own = lax.axis_index("beta") * cols + lax.broadcasted_iota(jnp.int32, (2, cols), 1)
    extra = lax.broadcasted_iota(jnp.int32, (2, cols), 0) + pairs + 2
    extra = own * 256 + extra * 2 + 1
    blank = jnp.zeros((LANES - nexc - 2, cols), jnp.int32)
    code = jnp.concatenate([code, extra, blank], axis=0).astype(f32)
    turned[...] = jnp.zeros_like(turned)
    for c in range(cols // LANES):
        turned[c * LANES : (c + 1) * LANES, :] = code[:, c * LANES : (c + 1) * LANES].T
    total = jnp.zeros((tiles, LANES), f32)
    for m in range(GROUP):
        part = turned[pl.ds(m, tiles, stride=GROUP), :]
        total += pltpu.roll(part, m * per_tile, 1) if m else part
    total = total.astype(jnp.int32)
    beta_ref[...] = total
    member = lax.div(lax.broadcasted_iota(jnp.int32, (tiles, LANES), 1), per_tile)
    slot = ((total >> 1) & 127) + LANES * member + 1
    slot = jnp.where((total & 1) == 1, slot, -slot).astype(f32)
    turned[:LANES, :] = jnp.zeros((LANES, LANES), f32)
    turned[:tiles, :] = slot
    slot_ref[...] = turned[:LANES, :].T.astype(jnp.int32)

    code = jnp.concatenate(
        [alpha_target[...], jnp.zeros((LANES - nexc, rows), jnp.int32)], axis=0
    )
    turned[:rows, :] = code.astype(f32).T
    period = rows * nexc // LANES // 8
    step = period * LANES // nexc
    found = [jnp.zeros((8, LANES), f32) for w in range(period)]
    for j in range(step):
        part = turned[pl.ds(j, 8, stride=step), :]
        w, shift = divmod(j * nexc, LANES)
        part = pltpu.roll(part, shift, 1) if shift else part
        found[w] += jnp.where(lane >= shift, part, 0.0)
        if shift + nexc > LANES:
            found[w + 1] += jnp.where(lane < shift + nexc - LANES, part, 0.0)
    for w in range(period):
        alpha_ref[8 * w : 8 * w + 8, :] = found[w].astype(jnp.int32)


def scatter(s, first, last, sizes, alpha_ref, lifted):
    rows, nexc = sizes[1], sizes[3]
    base = (lax.axis_index("alpha") ^ s) * rows
    period = rows * nexc // LANES // 8
    b_ids = lax.broadcasted_iota(jnp.int32, (rows, LANES), 0)
    hots = []
    for tile in range(first * nexc // LANES, last * nexc // LANES):
        row = 8 * (tile % period) + tile // period
        target = alpha_ref[row : row + 1, :] - base
        hots.append(jnp.where(b_ids == target, 1.0, 0.0).astype(jnp.bfloat16))
    return jnp.dot(
        jnp.concatenate(hots, axis=1),
        lifted[first * nexc : last * nexc, :],
        preferred_element_type=jnp.float32,
    )


def pick(g, cols, beta_ref, c_refs, first, found):
    code = jnp.concatenate([beta_ref[2 * g : 2 * g + 1], beta_ref[2 * g + 1 : 2 * g + 2]], axis=1)
    target = code >> 8
    low = lax.rem(target, cols)
    high = lax.div(target, cols) ^ lax.axis_index("beta")
    j_ids = lax.broadcasted_iota(jnp.int32, (cols, 2 * LANES), 0)
    hot = jnp.where(j_ids == low, 1.0, 0.0).astype(jnp.bfloat16)
    for k, c_ref in enumerate(c_refs):
        here = jnp.dot(c_ref[...], hot, preferred_element_type=jnp.float32)
        found = here if found is None else jnp.where(high == first + k, here, found)
    return found


def early_kernel(cols, beta_ref, *rest):
    c_refs, early_ref = rest[:-1], rest[-1]
    for g in range(early_ref.shape[0]):
        early_ref[g] = pick(g, cols, beta_ref, c_refs, 0, None)


def far_kernel(sizes, beta_ref, slot_ref, alpha_ref, weights, early_ref, *rest):
    chunks, rows, cols, nexc, depth, blocks, stride = sizes
    c_refs, rest = rest[: chunks - EARLY], rest[chunks - EARLY :]
    lifted, same = rest[:2]
    out_refs, (density, picked, sums) = rest[2:-3], rest[-3:]
    per_tile = LANES // GROUP
    bf16, f32 = jnp.bfloat16, jnp.float32
    groups = early_ref.shape[0]

    for g in range(groups):
        found = pick(g, cols, beta_ref, c_refs, EARLY, early_ref[g])
        picked[g] = found.astype(bf16)

    ids = lax.broadcasted_iota(jnp.int32, (LANES, LANES), 1) + 1
    for t in range(2 * groups):
        slot = jnp.broadcast_to(slot_ref[:, t : t + 1], (LANES, LANES))
        value = jnp.where(slot > 0, 1.0, -1.0)
        slot = jnp.abs(slot)
        hots = []
        for m in range(GROUP):
            low = m * per_tile // 16 * 16
            high = min(-(-(m + 1) * per_tile // 16) * 16, LANES)
            part = slot[low:high] == ids[low:high] + m * LANES
            part = [jnp.where(part, value[low:high], 0.0).astype(bf16)]
            if low:
                part.insert(0, jnp.zeros((low, LANES), bf16))
            if high < LANES:
                part.append(jnp.zeros((LANES - high, LANES), bf16))
            hots.append(jnp.concatenate(part, axis=0))
        span = slice(t % 2 * LANES, (t % 2 + 1) * LANES)
        d = jnp.dot(
            picked[t // 2, :, span],
            jnp.concatenate(hots, axis=1),
            preferred_element_type=f32,
        )
        for m in range(GROUP):
            i = t * GROUP + m
            density[i * stride : i * stride + rows, :] = d[:, m * LANES : (m + 1) * LANES]

    for first in range(0, rows, BATCH):
        for a in range(first, first + BATCH, 2):
            parts = []
            for m in range(2):
                d = density[pl.ds(a + m, cols, stride=stride), :].T.astype(bf16)
                u = weights[(a + m) * depth : (a + m + 1) * depth, :]
                l = jnp.dot(u, d, preferred_element_type=f32)
                same[a + m : a + m + 1, :] = l[nexc : nexc + 1] + l[nexc + 1 : nexc + 2]
                parts.append(l[:nexc])
            lifted[a * nexc : (a + 2) * nexc, :] = jnp.concatenate(parts, axis=0).astype(bf16)
        for s in range(blocks // 2):
            part = scatter(blocks // 2 + s, first, first + BATCH, sizes, alpha_ref, lifted)
            if first:
                part += sums[s]
            if first + BATCH < rows:
                sums[s] = part
            else:
                out_refs[s][...] = part.astype(bf16)


def near_kernel(sizes, alpha_ref, lifted, *out_refs):
    for s, out_ref in enumerate(out_refs):
        total = scatter(s + 1, 0, sizes[1], sizes, alpha_ref, lifted)
        out_ref[...] = total.astype(jnp.bfloat16)


def own_kernel(sizes, alpha_ref, lifted, same, own_ref):
    own_ref[...] = scatter(0, 0, sizes[1], sizes, alpha_ref, lifted) + same[...]


def shards(
    ci_vector,
    one_body,
    pair_integrals,
    beta_target,
    beta_pair,
    beta_sign,
    alpha_target,
    alpha_pair,
    alpha_sign,
):
    rows, cols = ci_vector.shape
    pairs = one_body.shape[0]
    nexc = beta_target.shape[0]
    blocks = lax.axis_size("alpha")
    chunks = lax.axis_size("beta")
    bf16 = jnp.bfloat16

    civec_bf = ci_vector.astype(bf16)
    gathered = [civec_bf] + [
        lax.ppermute(civec_bf, "beta", [(d, d ^ s) for d in range(chunks)])
        for s in range(1, chunks)
    ]

    depth = nexc + 8
    tiles = -(-cols // (2 * GROUP)) * 2
    vmem = pl.BlockSpec(memory_space=pltpu.VMEM)
    lists = (
        beta_target,
        beta_pair,
        beta_sign,
        alpha_target,
        alpha_pair,
        alpha_sign,
        one_body.reshape(1, pairs),
        pair_integrals,
    )
    beta_code, beta_slot, alpha_code, weights = pl.pallas_call(
        functools.partial(index_kernel, (rows, cols, nexc, depth, tiles, pairs)),
        out_shape=[
            pltpu.VMEM((tiles, LANES), jnp.int32),
            pltpu.VMEM((LANES, LANES), jnp.int32),
            pltpu.VMEM((rows * nexc // LANES, LANES), jnp.int32),
            pltpu.VMEM((rows * depth, LANES), bf16),
        ],
        in_specs=[pl.BlockSpec(memory_space=pltpu.HBM)] * 8,
        out_specs=[vmem] * 4,
        scratch_shapes=[pltpu.VMEM(x.shape, x.dtype) for x in lists]
        + [
            pltpu.VMEM((LANES, LANES), jnp.float32),
            pltpu.VMEM((tiles * GROUP, LANES), jnp.float32),
            pltpu.SemaphoreType.DMA((len(lists),)),
        ],
        cost_estimate=pl.CostEstimate(
            flops=4 * rows * depth * LANES * LANES, bytes_accessed=0, transcendentals=0
        ),
        compiler_params=pltpu.CompilerParams(vmem_limit_bytes=16 * 1024 * 1024),
        name="index_lists",
    )(*[pltpu.with_memory_space_constraint(x, pltpu.HBM) for x in lists])

    stride = rows + 4
    early = pl.pallas_call(
        functools.partial(early_kernel, cols),
        out_shape=pltpu.VMEM((tiles // 2, rows, 2 * LANES), jnp.float32),
        in_specs=[vmem] * (1 + EARLY),
        out_specs=vmem,
        compiler_params=pltpu.CompilerParams(vmem_limit_bytes=12 * 1024 * 1024),
        cost_estimate=pl.CostEstimate(
            flops=4 * rows * cols * tiles * LANES, bytes_accessed=0, transcendentals=0
        ),
        name="gather_early",
    )(beta_code, *gathered[:EARLY])
    sizes = (chunks, rows, cols, nexc, depth, blocks, stride)
    block = jax.ShapeDtypeStruct((rows, cols), bf16)
    block_f32 = jax.ShapeDtypeStruct((rows, cols), jnp.float32)
    lifted, same, *far = pl.pallas_call(
        functools.partial(far_kernel, sizes),
        out_shape=[jax.ShapeDtypeStruct((rows * nexc, cols), bf16), block_f32]
        + [block] * (blocks // 2),
        in_specs=[vmem] * (5 + chunks - EARLY),
        out_specs=[vmem] * (2 + blocks // 2),
        scratch_shapes=[
            pltpu.VMEM((tiles * GROUP * stride, LANES), jnp.float32),
            pltpu.VMEM((tiles // 2, rows, 2 * LANES), bf16),
            pltpu.VMEM((blocks // 2, rows, cols), jnp.float32),
        ],
        compiler_params=pltpu.CompilerParams(vmem_limit_bytes=36 * 1024 * 1024),
        name="sigma_far",
    )(beta_code, beta_slot, alpha_code, weights, early, *gathered[EARLY:])

    def send(s, value):
        return lax.ppermute(value, "alpha", [(d, d ^ s) for d in range(blocks)])

    far_sum = far[0].astype(jnp.float32)
    for s in reversed(range(1, blocks // 2)):
        far_sum = far_sum + send(s, far[s]).astype(jnp.float32)
    far_sum = far_sum.astype(bf16)
    near = pl.pallas_call(
        functools.partial(near_kernel, sizes),
        out_shape=[block] * (blocks // 2 - 1),
        in_specs=[vmem] * 2,
        out_specs=[vmem] * (blocks // 2 - 1),
        compiler_params=pltpu.CompilerParams(vmem_limit_bytes=8 * 1024 * 1024),
        cost_estimate=pl.CostEstimate(
            flops=(blocks - 2) * rows * rows * nexc * cols, bytes_accessed=0, transcendentals=0
        ),
        name="sigma_near",
    )(alpha_code, lifted)
    own = pl.pallas_call(
        functools.partial(own_kernel, sizes),
        out_shape=block_f32,
        in_specs=[vmem] * 3,
        out_specs=vmem,
        compiler_params=pltpu.CompilerParams(vmem_limit_bytes=4 * 1024 * 1024),
        cost_estimate=pl.CostEstimate(
            flops=2 * rows * rows * nexc * cols, bytes_accessed=0, transcendentals=0
        ),
        name="sigma_own",
    )(alpha_code, lifted, same)
    crossing = send(blocks // 2, far_sum)
    total = own
    for got in [send(s + 1, near[s]) for s in range(blocks // 2 - 1)] + [crossing]:
        total = total + got.astype(jnp.float32)
    return total


def solution(mesh):
    placed = (
        P("alpha", "beta"),
        P(),
        P(),
        P(None, "beta"),
        P(None, "beta"),
        P(None, "beta"),
        P(None, "alpha"),
        P(None, "alpha"),
        P(None, "alpha"),
    )
    return jax.shard_map(
        shards, mesh=mesh, in_specs=placed, out_specs=P("alpha", "beta"), check_vma=False
    )
```

```python
import functools

import jax
import jax.numpy as jnp
from jax import lax
from jax.experimental import pallas as pl
from jax.experimental.pallas import tpu as pltpu
from jax.sharding import PartitionSpec as P

LANES = 128
BATCH = 32
EARLY = 2
GROUP = 3
NT = (((1,), (1,)), ((), ()))


def stage_kernel(count, *refs):
    sources, (civec_ref, *staged) = refs[: count + 1], refs[count + 1 : 2 * count + 2]
    landing, arrived = refs[2 * count + 2 :]
    copies = [
        pltpu.make_async_copy(source, target, arrived.at[n])
        for n, (source, target) in enumerate(zip(sources, [landing, *staged]))
    ]
    for copy in copies:
        copy.start()
    copies[0].wait()
    civec_ref[...] = landing[...].astype(jnp.bfloat16)
    for copy in copies[1:]:
        copy.wait()


def index_kernel(
    sizes,
    beta_target,
    beta_pair,
    beta_sign,
    alpha_target,
    alpha_pair,
    alpha_sign,
    one_body,
    integrals,
    beta_ref,
    slot_ref,
    alpha_ref,
    weights_ref,
    table,
    turned,
):
    rows, cols, nexc, depth, tiles, pairs = sizes
    bf16, f32 = jnp.bfloat16, jnp.float32
    per_tile = LANES // GROUP
    lane = lax.broadcasted_iota(jnp.int32, (8, LANES), 1)

    h = one_body[...]
    h_high = h.astype(bf16).astype(f32)
    halves = jnp.concatenate([h_high, h - h_high], axis=0)
    table[...] = jnp.zeros_like(table)
    table[pairs + 2 : pairs + 4, :pairs] = halves
    columns = table[...].T
    table[...] = jnp.zeros_like(table)
    table[:pairs, :pairs] = integrals[...].astype(f32)
    table[pairs : pairs + 2, :pairs] = halves
    rows_of = (table[...] + columns).astype(bf16)

    signed = (2 * alpha_sign[...] - 1) * (alpha_pair[...] + 1)
    after = lax.broadcasted_iota(jnp.int32, (depth - nexc, rows), 0) + pairs + 1
    signed = jnp.concatenate([signed, after], axis=0)
    q_ids = lax.broadcasted_iota(jnp.int32, (depth, LANES), 1) + 1
    batch = 16
    for b in range(rows // batch):
        hots = []
        for a in range(b * batch, (b + 1) * batch):
            column = jnp.broadcast_to(signed[:, a : a + 1], (depth, LANES))
            value = jnp.where(column > 0, 1.0, -1.0)
            hots.append(jnp.where(jnp.abs(column) == q_ids, value, 0.0).astype(bf16))
        u = jnp.dot(jnp.concatenate(hots, axis=0), rows_of, preferred_element_type=f32)
        weights_ref[b * batch * depth : (b + 1) * batch * depth, :] = u.astype(bf16)

    code = beta_target[...] * 256 + beta_pair[...] * 2 + beta_sign[...]
    own = lax.axis_index("beta") * cols + lax.broadcasted_iota(jnp.int32, (2, cols), 1)
    extra = lax.broadcasted_iota(jnp.int32, (2, cols), 0) + pairs + 2
    extra = own * 256 + extra * 2 + 1
    blank = jnp.zeros((LANES - nexc - 2, cols), jnp.int32)
    code = jnp.concatenate([code, extra, blank], axis=0).astype(f32)
    turned[...] = jnp.zeros_like(turned)
    for c in range(cols // LANES):
        turned[c * LANES : (c + 1) * LANES, :] = code[:, c * LANES : (c + 1) * LANES].T
    total = jnp.zeros((tiles, LANES), f32)
    for m in range(GROUP):
        part = turned[pl.ds(m, tiles, stride=GROUP), :]
        total += pltpu.roll(part, m * per_tile, 1) if m else part
    total = total.astype(jnp.int32)
    beta_ref[...] = total
    member = lax.div(lax.broadcasted_iota(jnp.int32, (tiles, LANES), 1), per_tile)
    slot = ((total >> 1) & 127) + LANES * member + 1
    slot = jnp.where((total & 1) == 1, slot, -slot).astype(f32)
    turned[:LANES, :] = jnp.zeros((LANES, LANES), f32)
    turned[:tiles, :] = slot
    slot_ref[...] = turned[:LANES, :].T.astype(jnp.int32)

    code = jnp.concatenate(
        [alpha_target[...], jnp.zeros((LANES - nexc, rows), jnp.int32)], axis=0
    )
    turned[:rows, :] = code.astype(f32).T
    period = rows * nexc // LANES // 8
    step = period * LANES // nexc
    found = [jnp.zeros((8, LANES), f32) for w in range(period)]
    for j in range(step):
        part = turned[pl.ds(j, 8, stride=step), :]
        w, shift = divmod(j * nexc, LANES)
        part = pltpu.roll(part, shift, 1) if shift else part
        found[w] += jnp.where(lane >= shift, part, 0.0)
        if shift + nexc > LANES:
            found[w + 1] += jnp.where(lane < shift + nexc - LANES, part, 0.0)
    for w in range(period):
        alpha_ref[8 * w : 8 * w + 8, :] = found[w].astype(jnp.int32)


def scatter(s, first, last, sizes, alpha_ref, lifted):
    rows, nexc = sizes[1], sizes[3]
    base = (lax.axis_index("alpha") ^ s) * rows
    period = rows * nexc // LANES // 8
    b_ids = lax.broadcasted_iota(jnp.int32, (rows, LANES), 0)
    hots = []
    for tile in range(first * nexc // LANES, last * nexc // LANES):
        row = 8 * (tile % period) + tile // period
        target = alpha_ref[row : row + 1, :] - base
        hots.append(jnp.where(b_ids == target, 1.0, 0.0).astype(jnp.bfloat16))
    return jnp.dot(
        jnp.concatenate(hots, axis=1),
        lifted[first * nexc : last * nexc, :],
        preferred_element_type=jnp.float32,
    )


def pick(g, cols, beta_ref, c_refs, first, found):
    code = jnp.concatenate([beta_ref[2 * g : 2 * g + 1], beta_ref[2 * g + 1 : 2 * g + 2]], axis=1)
    target = code >> 8
    low = lax.rem(target, cols)
    high = lax.div(target, cols) ^ lax.axis_index("beta")
    j_ids = lax.broadcasted_iota(jnp.int32, (cols, 2 * LANES), 0)
    hot = jnp.where(j_ids == low, 1.0, 0.0).astype(jnp.bfloat16)
    for k, c_ref in enumerate(c_refs):
        here = jnp.dot(c_ref[...], hot, preferred_element_type=jnp.float32)
        found = here if found is None else jnp.where(high == first + k, here, found)
    return found


def early_kernel(cols, beta_ref, *rest):
    c_refs, early_ref = rest[:-1], rest[-1]
    for g in range(early_ref.shape[0]):
        early_ref[g] = pick(g, cols, beta_ref, c_refs, 0, None)


def far_kernel(sizes, beta_ref, slot_ref, alpha_ref, weights, early_ref, *rest):
    chunks, rows, cols, nexc, depth, blocks, stride = sizes
    c_refs, rest = rest[: chunks - EARLY], rest[chunks - EARLY :]
    lifted, same = rest[:2]
    out_refs, (density, picked, sums) = rest[2:-3], rest[-3:]
    per_tile = LANES // GROUP
    bf16, f32 = jnp.bfloat16, jnp.float32
    groups = early_ref.shape[0]

    for g in range(groups):
        found = pick(g, cols, beta_ref, c_refs, EARLY, early_ref[g])
        picked[g] = found.astype(bf16)

    ids = lax.broadcasted_iota(jnp.int32, (LANES, LANES), 1) + 1
    for t in range(2 * groups):
        slot = jnp.broadcast_to(slot_ref[:, t : t + 1], (LANES, LANES))
        value = jnp.where(slot > 0, 1.0, -1.0)
        slot = jnp.abs(slot)
        hots = []
        for m in range(GROUP):
            low = m * per_tile // 16 * 16
            high = min(-(-(m + 1) * per_tile // 16) * 16, LANES)
            part = slot[low:high] == ids[low:high] + m * LANES
            part = [jnp.where(part, value[low:high], 0.0).astype(bf16)]
            if low:
                part.insert(0, jnp.zeros((low, LANES), bf16))
            if high < LANES:
                part.append(jnp.zeros((LANES - high, LANES), bf16))
            hots.append(jnp.concatenate(part, axis=0))
        span = slice(t % 2 * LANES, (t % 2 + 1) * LANES)
        d = jnp.dot(
            picked[t // 2, :, span],
            jnp.concatenate(hots, axis=1),
            preferred_element_type=f32,
        )
        for m in range(GROUP):
            i = t * GROUP + m
            density[i * stride : i * stride + rows, :] = d[:, m * LANES : (m + 1) * LANES]

    for first in range(0, rows, BATCH):
        for a in range(first, first + BATCH, 2):
            parts = []
            for m in range(2):
                d = density[pl.ds(a + m, cols, stride=stride), :].T.astype(bf16)
                u = weights[(a + m) * depth : (a + m + 1) * depth, :]
                l = jnp.dot(u, d, preferred_element_type=f32)
                same[a + m : a + m + 1, :] = l[nexc : nexc + 1] + l[nexc + 1 : nexc + 2]
                parts.append(l[:nexc])
            lifted[a * nexc : (a + 2) * nexc, :] = jnp.concatenate(parts, axis=0).astype(bf16)
        for s in range(blocks // 2):
            part = scatter(blocks // 2 + s, first, first + BATCH, sizes, alpha_ref, lifted)
            if first:
                part += sums[s]
            if first + BATCH < rows:
                sums[s] = part
            else:
                out_refs[s][...] = part.astype(bf16)


def near_kernel(sizes, alpha_ref, lifted, *out_refs):
    for s, out_ref in enumerate(out_refs):
        total = scatter(s + 1, 0, sizes[1], sizes, alpha_ref, lifted)
        out_ref[...] = total.astype(jnp.bfloat16)


def own_kernel(sizes, alpha_ref, lifted, same, own_ref):
    own_ref[...] = scatter(0, 0, sizes[1], sizes, alpha_ref, lifted) + same[...]


def shards(
    ci_vector,
    one_body,
    pair_integrals,
    beta_target,
    beta_pair,
    beta_sign,
    alpha_target,
    alpha_pair,
    alpha_sign,
):
    rows, cols = ci_vector.shape
    pairs = one_body.shape[0]
    nexc = beta_target.shape[0]
    blocks = lax.axis_size("alpha")
    chunks = lax.axis_size("beta")
    bf16 = jnp.bfloat16

    lists = (
        beta_target,
        beta_pair,
        beta_sign,
        alpha_target,
        alpha_pair,
        alpha_sign,
        one_body.reshape(1, pairs),
        pair_integrals,
    )
    vmem = pl.BlockSpec(memory_space=pltpu.VMEM)
    civec_bf, *lists = pl.pallas_call(
        functools.partial(stage_kernel, len(lists)),
        out_shape=[pltpu.VMEM((rows, cols), bf16)] + [pltpu.VMEM(x.shape, x.dtype) for x in lists],
        in_specs=[pl.BlockSpec(memory_space=pltpu.HBM)] * (1 + len(lists)),
        out_specs=[vmem] * (1 + len(lists)),
        scratch_shapes=[
            pltpu.VMEM((rows, cols), jnp.float32),
            pltpu.SemaphoreType.DMA((1 + len(lists),)),
        ],
        compiler_params=pltpu.CompilerParams(vmem_limit_bytes=4 * 1024 * 1024),
        name="stage",
    )(*[pltpu.with_memory_space_constraint(x, pltpu.HBM) for x in (ci_vector, *lists)])
    gathered = [civec_bf] + [
        lax.ppermute(civec_bf, "beta", [(d, d ^ s) for d in range(chunks)])
        for s in range(1, chunks)
    ]

    depth = nexc + 8
    tiles = -(-cols // (2 * GROUP)) * 2
    beta_code, beta_slot, alpha_code, weights = pl.pallas_call(
        functools.partial(index_kernel, (rows, cols, nexc, depth, tiles, pairs)),
        out_shape=[
            pltpu.VMEM((tiles, LANES), jnp.int32),
            pltpu.VMEM((LANES, LANES), jnp.int32),
            pltpu.VMEM((rows * nexc // LANES, LANES), jnp.int32),
            pltpu.VMEM((rows * depth, LANES), bf16),
        ],
        in_specs=[vmem] * 8,
        out_specs=[vmem] * 4,
        scratch_shapes=[
            pltpu.VMEM((LANES, LANES), jnp.float32),
            pltpu.VMEM((tiles * GROUP, LANES), jnp.float32),
        ],
        cost_estimate=pl.CostEstimate(
            flops=4 * rows * depth * LANES * LANES, bytes_accessed=0, transcendentals=0
        ),
        compiler_params=pltpu.CompilerParams(vmem_limit_bytes=16 * 1024 * 1024),
        name="index_lists",
    )(*lists)

    stride = rows + 4
    early = pl.pallas_call(
        functools.partial(early_kernel, cols),
        out_shape=pltpu.VMEM((tiles // 2, rows, 2 * LANES), jnp.float32),
        in_specs=[vmem] * (1 + EARLY),
        out_specs=vmem,
        compiler_params=pltpu.CompilerParams(vmem_limit_bytes=12 * 1024 * 1024),
        cost_estimate=pl.CostEstimate(
            flops=4 * rows * cols * tiles * LANES, bytes_accessed=0, transcendentals=0
        ),
        name="gather_early",
    )(beta_code, *gathered[:EARLY])
    sizes = (chunks, rows, cols, nexc, depth, blocks, stride)
    block = jax.ShapeDtypeStruct((rows, cols), bf16)
    block_f32 = jax.ShapeDtypeStruct((rows, cols), jnp.float32)
    lifted, same, *far = pl.pallas_call(
        functools.partial(far_kernel, sizes),
        out_shape=[jax.ShapeDtypeStruct((rows * nexc, cols), bf16), block_f32]
        + [block] * (blocks // 2),
        in_specs=[vmem] * (5 + chunks - EARLY),
        out_specs=[vmem] * (2 + blocks // 2),
        scratch_shapes=[
            pltpu.VMEM((tiles * GROUP * stride, LANES), jnp.float32),
            pltpu.VMEM((tiles // 2, rows, 2 * LANES), bf16),
            pltpu.VMEM((blocks // 2, rows, cols), jnp.float32),
        ],
        compiler_params=pltpu.CompilerParams(vmem_limit_bytes=36 * 1024 * 1024),
        name="sigma_far",
    )(beta_code, beta_slot, alpha_code, weights, early, *gathered[EARLY:])

    def send(s, value):
        return lax.ppermute(value, "alpha", [(d, d ^ s) for d in range(blocks)])

    far_sum = far[0].astype(jnp.float32)
    for s in reversed(range(1, blocks // 2)):
        far_sum = far_sum + send(s, far[s]).astype(jnp.float32)
    far_sum = far_sum.astype(bf16)
    near = pl.pallas_call(
        functools.partial(near_kernel, sizes),
        out_shape=[block] * (blocks // 2 - 1),
        in_specs=[vmem] * 2,
        out_specs=[vmem] * (blocks // 2 - 1),
        compiler_params=pltpu.CompilerParams(vmem_limit_bytes=8 * 1024 * 1024),
        cost_estimate=pl.CostEstimate(
            flops=(blocks - 2) * rows * rows * nexc * cols, bytes_accessed=0, transcendentals=0
        ),
        name="sigma_near",
    )(alpha_code, lifted)
    own = pl.pallas_call(
        functools.partial(own_kernel, sizes),
        out_shape=block_f32,
        in_specs=[vmem] * 3,
        out_specs=vmem,
        compiler_params=pltpu.CompilerParams(vmem_limit_bytes=4 * 1024 * 1024),
        cost_estimate=pl.CostEstimate(
            flops=2 * rows * rows * nexc * cols, bytes_accessed=0, transcendentals=0
        ),
        name="sigma_own",
    )(alpha_code, lifted, same)
    crossing = send(blocks // 2, far_sum)
    total = own
    for got in [send(s + 1, near[s]) for s in range(blocks // 2 - 1)] + [crossing]:
        total = total + got.astype(jnp.float32)
    return total


def solution(mesh):
    placed = (
        P("alpha", "beta"),
        P(),
        P(),
        P(None, "beta"),
        P(None, "beta"),
        P(None, "beta"),
        P(None, "alpha"),
        P(None, "alpha"),
        P(None, "alpha"),
    )
    return jax.shard_map(
        shards, mesh=mesh, in_specs=placed, out_specs=P("alpha", "beta"), check_vma=False
    )
```

```python
import functools

import jax
import jax.numpy as jnp
from jax import lax
from jax.experimental import pallas as pl
from jax.experimental.pallas import tpu as pltpu
from jax.sharding import PartitionSpec as P

LANES = 128
BATCH = 32
EARLY = 2
GROUP = 3
NT = (((1,), (1,)), ((), ()))


def stage_kernel(count, *refs):
    sources, (civec_ref, *staged) = refs[: count + 1], refs[count + 1 : 2 * count + 2]
    landing, arrived = refs[2 * count + 2 :]
    copies = [
        pltpu.make_async_copy(source, target, arrived.at[n])
        for n, (source, target) in enumerate(zip(sources, [landing, *staged]))
    ]
    for copy in copies:
        copy.start()
    copies[0].wait()
    civec_ref[...] = landing[...].astype(jnp.bfloat16)
    for copy in copies[1:]:
        copy.wait()


def index_kernel(
    sizes,
    beta_target,
    beta_pair,
    beta_sign,
    alpha_target,
    alpha_pair,
    alpha_sign,
    one_body,
    integrals,
    beta_ref,
    slot_ref,
    alpha_ref,
    weights_ref,
    table,
    turned,
):
    rows, cols, nexc, depth, tiles, pairs = sizes
    bf16, f32 = jnp.bfloat16, jnp.float32
    per_tile = LANES // GROUP
    lane = lax.broadcasted_iota(jnp.int32, (8, LANES), 1)

    h = one_body[...]
    h_high = h.astype(bf16).astype(f32)
    halves = jnp.concatenate([h_high, h - h_high], axis=0)
    table[...] = jnp.zeros_like(table)
    table[pairs + 2 : pairs + 4, :pairs] = halves
    columns = table[...].T
    table[...] = jnp.zeros_like(table)
    table[:pairs, :pairs] = integrals[...].astype(f32)
    table[pairs : pairs + 2, :pairs] = halves
    rows_of = (table[...] + columns).astype(bf16)

    signed = (2 * alpha_sign[...] - 1) * (alpha_pair[...] + 1)
    after = lax.broadcasted_iota(jnp.int32, (depth - nexc, rows), 0) + pairs + 1
    signed = jnp.concatenate([signed, after], axis=0)
    q_ids = lax.broadcasted_iota(jnp.int32, (depth, LANES), 1) + 1
    batch = 16
    for b in range(rows // batch):
        hots = []
        for a in range(b * batch, (b + 1) * batch):
            column = jnp.broadcast_to(signed[:, a : a + 1], (depth, LANES))
            value = jnp.where(column > 0, 1.0, -1.0)
            hots.append(jnp.where(jnp.abs(column) == q_ids, value, 0.0).astype(bf16))
        u = jnp.dot(jnp.concatenate(hots, axis=0), rows_of, preferred_element_type=f32)
        weights_ref[b * batch * depth : (b + 1) * batch * depth, :] = u.astype(bf16)

    code = beta_target[...] * 256 + beta_pair[...] * 2 + beta_sign[...]
    own = lax.axis_index("beta") * cols + lax.broadcasted_iota(jnp.int32, (2, cols), 1)
    extra = lax.broadcasted_iota(jnp.int32, (2, cols), 0) + pairs + 2
    extra = own * 256 + extra * 2 + 1
    blank = jnp.zeros((LANES - nexc - 2, cols), jnp.int32)
    code = jnp.concatenate([code, extra, blank], axis=0).astype(f32)
    turned[...] = jnp.zeros_like(turned)
    for c in range(cols // LANES):
        turned[c * LANES : (c + 1) * LANES, :] = code[:, c * LANES : (c + 1) * LANES].T
    total = jnp.zeros((tiles, LANES), f32)
    for m in range(GROUP):
        part = turned[pl.ds(m, tiles, stride=GROUP), :]
        total += pltpu.roll(part, m * per_tile, 1) if m else part
    total = total.astype(jnp.int32)
    beta_ref[...] = total
    member = lax.div(lax.broadcasted_iota(jnp.int32, (tiles, LANES), 1), per_tile)
    slot = ((total >> 1) & 127) + LANES * member + 1
    slot = jnp.where((total & 1) == 1, slot, -slot).astype(f32)
    turned[:LANES, :] = jnp.zeros((LANES, LANES), f32)
    turned[:tiles, :] = slot
    slot_ref[...] = turned[:LANES, :].T.astype(jnp.int32)

    code = jnp.concatenate(
        [alpha_target[...], jnp.zeros((LANES - nexc, rows), jnp.int32)], axis=0
    )
    turned[:rows, :] = code.astype(f32).T
    period = rows * nexc // LANES // 8
    step = period * LANES // nexc
    found = [jnp.zeros((8, LANES), f32) for w in range(period)]
    for j in range(step):
        part = turned[pl.ds(j, 8, stride=step), :]
        w, shift = divmod(j * nexc, LANES)
        part = pltpu.roll(part, shift, 1) if shift else part
        found[w] += jnp.where(lane >= shift, part, 0.0)
        if shift + nexc > LANES:
            found[w + 1] += jnp.where(lane < shift + nexc - LANES, part, 0.0)
    for w in range(period):
        alpha_ref[8 * w : 8 * w + 8, :] = found[w].astype(jnp.int32)


def scatter(s, first, last, sizes, alpha_ref, lifted):
    rows, nexc = sizes[1], sizes[3]
    base = (lax.axis_index("alpha") ^ s) * rows
    period = rows * nexc // LANES // 8
    b_ids = lax.broadcasted_iota(jnp.int32, (rows, LANES), 0)
    hots = []
    for tile in range(first * nexc // LANES, last * nexc // LANES):
        row = 8 * (tile % period) + tile // period
        target = alpha_ref[row : row + 1, :] - base
        hots.append(jnp.where(b_ids == target, 1.0, 0.0).astype(jnp.bfloat16))
    return jnp.dot(
        jnp.concatenate(hots, axis=1),
        lifted[first * nexc : last * nexc, :],
        preferred_element_type=jnp.float32,
    )


def pick(g, cols, beta_ref, c_refs, first, found):
    code = jnp.concatenate([beta_ref[2 * g : 2 * g + 1], beta_ref[2 * g + 1 : 2 * g + 2]], axis=1)
    target = code >> 8
    low = lax.rem(target, cols)
    high = lax.div(target, cols) ^ lax.axis_index("beta")
    j_ids = lax.broadcasted_iota(jnp.int32, (cols, 2 * LANES), 0)
    hot = jnp.where(j_ids == low, 1.0, 0.0).astype(jnp.bfloat16)
    for k, c_ref in enumerate(c_refs):
        here = jnp.dot(c_ref[...], hot, preferred_element_type=jnp.float32)
        found = here if found is None else jnp.where(high == first + k, here, found)
    return found


def early_kernel(cols, beta_ref, *rest):
    c_refs, early_ref = rest[:-1], rest[-1]
    for g in range(early_ref.shape[0]):
        early_ref[g] = pick(g, cols, beta_ref, c_refs, 0, None)


def far_kernel(sizes, beta_ref, slot_ref, alpha_ref, weights, early_ref, *rest):
    chunks, rows, cols, nexc, depth, blocks, stride = sizes
    c_refs, rest = rest[: chunks - EARLY], rest[chunks - EARLY :]
    lifted, same = rest[:2]
    out_refs, (density, picked, sums) = rest[2:-3], rest[-3:]
    per_tile = LANES // GROUP
    bf16, f32 = jnp.bfloat16, jnp.float32
    groups = early_ref.shape[0]

    for g in range(groups):
        found = pick(g, cols, beta_ref, c_refs, EARLY, early_ref[g])
        picked[g] = found.astype(bf16)

    ids = lax.broadcasted_iota(jnp.int32, (LANES, LANES), 1) + 1
    for t in range(2 * groups):
        slot = jnp.broadcast_to(slot_ref[:, t : t + 1], (LANES, LANES))
        value = jnp.where(slot > 0, 1.0, -1.0)
        slot = jnp.abs(slot)
        hots = []
        for m in range(GROUP):
            low = m * per_tile // 16 * 16
            high = min(-(-(m + 1) * per_tile // 16) * 16, LANES)
            part = slot[low:high] == ids[low:high] + m * LANES
            part = [jnp.where(part, value[low:high], 0.0).astype(bf16)]
            if low:
                part.insert(0, jnp.zeros((low, LANES), bf16))
            if high < LANES:
                part.append(jnp.zeros((LANES - high, LANES), bf16))
            hots.append(jnp.concatenate(part, axis=0))
        span = slice(t % 2 * LANES, (t % 2 + 1) * LANES)
        d = jnp.dot(
            picked[t // 2, :, span],
            jnp.concatenate(hots, axis=1),
            preferred_element_type=f32,
        )
        for m in range(GROUP):
            i = t * GROUP + m
            density[i * stride : i * stride + rows, :] = d[:, m * LANES : (m + 1) * LANES]

    for first in range(0, rows, BATCH):
        for a in range(first, first + BATCH, 2):
            parts = []
            for m in range(2):
                d = density[pl.ds(a + m, cols, stride=stride), :]
                u = weights[(a + m) * depth : (a + m + 1) * depth, :]
                if m and a % 4:
                    l = lax.dot_general(u, d.astype(bf16), NT, preferred_element_type=f32)
                else:
                    l = jnp.dot(u, d.T.astype(bf16), preferred_element_type=f32)
                same[a + m : a + m + 1, :] = l[nexc : nexc + 1] + l[nexc + 1 : nexc + 2]
                parts.append(l[:nexc])
            lifted[a * nexc : (a + 2) * nexc, :] = jnp.concatenate(parts, axis=0).astype(bf16)
        for s in range(blocks // 2):
            part = scatter(blocks // 2 + s, first, first + BATCH, sizes, alpha_ref, lifted)
            if first:
                part += sums[s]
            if first + BATCH < rows:
                sums[s] = part
            else:
                out_refs[s][...] = part.astype(bf16)


def near_kernel(sizes, alpha_ref, lifted, *out_refs):
    for s, out_ref in enumerate(out_refs):
        total = scatter(s + 1, 0, sizes[1], sizes, alpha_ref, lifted)
        out_ref[...] = total.astype(jnp.bfloat16)


def own_kernel(sizes, alpha_ref, lifted, same, own_ref):
    own_ref[...] = scatter(0, 0, sizes[1], sizes, alpha_ref, lifted) + same[...]


def shards(
    ci_vector,
    one_body,
    pair_integrals,
    beta_target,
    beta_pair,
    beta_sign,
    alpha_target,
    alpha_pair,
    alpha_sign,
):
    rows, cols = ci_vector.shape
    pairs = one_body.shape[0]
    nexc = beta_target.shape[0]
    blocks = lax.axis_size("alpha")
    chunks = lax.axis_size("beta")
    bf16 = jnp.bfloat16

    lists = (
        beta_target,
        beta_pair,
        beta_sign,
        alpha_target,
        alpha_pair,
        alpha_sign,
        one_body.reshape(1, pairs),
        pair_integrals,
    )
    vmem = pl.BlockSpec(memory_space=pltpu.VMEM)
    civec_bf, *lists = pl.pallas_call(
        functools.partial(stage_kernel, len(lists)),
        out_shape=[pltpu.VMEM((rows, cols), bf16)] + [pltpu.VMEM(x.shape, x.dtype) for x in lists],
        in_specs=[pl.BlockSpec(memory_space=pltpu.HBM)] * (1 + len(lists)),
        out_specs=[vmem] * (1 + len(lists)),
        scratch_shapes=[
            pltpu.VMEM((rows, cols), jnp.float32),
            pltpu.SemaphoreType.DMA((1 + len(lists),)),
        ],
        compiler_params=pltpu.CompilerParams(vmem_limit_bytes=4 * 1024 * 1024),
        name="stage",
    )(*[pltpu.with_memory_space_constraint(x, pltpu.HBM) for x in (ci_vector, *lists)])
    gathered = [civec_bf] + [
        lax.ppermute(civec_bf, "beta", [(d, d ^ s) for d in range(chunks)])
        for s in range(1, chunks)
    ]

    depth = nexc + 8
    tiles = -(-cols // (2 * GROUP)) * 2
    beta_code, beta_slot, alpha_code, weights = pl.pallas_call(
        functools.partial(index_kernel, (rows, cols, nexc, depth, tiles, pairs)),
        out_shape=[
            pltpu.VMEM((tiles, LANES), jnp.int32),
            pltpu.VMEM((LANES, LANES), jnp.int32),
            pltpu.VMEM((rows * nexc // LANES, LANES), jnp.int32),
            pltpu.VMEM((rows * depth, LANES), bf16),
        ],
        in_specs=[vmem] * 8,
        out_specs=[vmem] * 4,
        scratch_shapes=[
            pltpu.VMEM((LANES, LANES), jnp.float32),
            pltpu.VMEM((tiles * GROUP, LANES), jnp.float32),
        ],
        cost_estimate=pl.CostEstimate(
            flops=4 * rows * depth * LANES * LANES, bytes_accessed=0, transcendentals=0
        ),
        compiler_params=pltpu.CompilerParams(vmem_limit_bytes=16 * 1024 * 1024),
        name="index_lists",
    )(*lists)

    stride = rows + 4
    early = pl.pallas_call(
        functools.partial(early_kernel, cols),
        out_shape=pltpu.VMEM((tiles // 2, rows, 2 * LANES), jnp.float32),
        in_specs=[vmem] * (1 + EARLY),
        out_specs=vmem,
        compiler_params=pltpu.CompilerParams(vmem_limit_bytes=12 * 1024 * 1024),
        cost_estimate=pl.CostEstimate(
            flops=4 * rows * cols * tiles * LANES, bytes_accessed=0, transcendentals=0
        ),
        name="gather_early",
    )(beta_code, *gathered[:EARLY])
    sizes = (chunks, rows, cols, nexc, depth, blocks, stride)
    block = jax.ShapeDtypeStruct((rows, cols), bf16)
    block_f32 = jax.ShapeDtypeStruct((rows, cols), jnp.float32)
    lifted, same, *far = pl.pallas_call(
        functools.partial(far_kernel, sizes),
        out_shape=[jax.ShapeDtypeStruct((rows * nexc, cols), bf16), block_f32]
        + [block] * (blocks // 2),
        in_specs=[vmem] * (5 + chunks - EARLY),
        out_specs=[vmem] * (2 + blocks // 2),
        scratch_shapes=[
            pltpu.VMEM((tiles * GROUP * stride, LANES), jnp.float32),
            pltpu.VMEM((tiles // 2, rows, 2 * LANES), bf16),
            pltpu.VMEM((blocks // 2, rows, cols), jnp.float32),
        ],
        compiler_params=pltpu.CompilerParams(vmem_limit_bytes=36 * 1024 * 1024),
        name="sigma_far",
    )(beta_code, beta_slot, alpha_code, weights, early, *gathered[EARLY:])

    def send(s, value):
        return lax.ppermute(value, "alpha", [(d, d ^ s) for d in range(blocks)])

    far_sum = far[0].astype(jnp.float32)
    for s in reversed(range(1, blocks // 2)):
        far_sum = far_sum + send(s, far[s]).astype(jnp.float32)
    far_sum = far_sum.astype(bf16)
    near = pl.pallas_call(
        functools.partial(near_kernel, sizes),
        out_shape=[block] * (blocks // 2 - 1),
        in_specs=[vmem] * 2,
        out_specs=[vmem] * (blocks // 2 - 1),
        compiler_params=pltpu.CompilerParams(vmem_limit_bytes=8 * 1024 * 1024),
        cost_estimate=pl.CostEstimate(
            flops=(blocks - 2) * rows * rows * nexc * cols, bytes_accessed=0, transcendentals=0
        ),
        name="sigma_near",
    )(alpha_code, lifted)
    own = pl.pallas_call(
        functools.partial(own_kernel, sizes),
        out_shape=block_f32,
        in_specs=[vmem] * 3,
        out_specs=vmem,
        compiler_params=pltpu.CompilerParams(vmem_limit_bytes=4 * 1024 * 1024),
        cost_estimate=pl.CostEstimate(
            flops=2 * rows * rows * nexc * cols, bytes_accessed=0, transcendentals=0
        ),
        name="sigma_own",
    )(alpha_code, lifted, same)
    crossing = send(blocks // 2, far_sum)
    total = own
    for got in [send(s + 1, near[s]) for s in range(blocks // 2 - 1)] + [crossing]:
        total = total + got.astype(jnp.float32)
    return total


def solution(mesh):
    placed = (
        P("alpha", "beta"),
        P(),
        P(),
        P(None, "beta"),
        P(None, "beta"),
        P(None, "beta"),
        P(None, "alpha"),
        P(None, "alpha"),
        P(None, "alpha"),
    )
    return jax.shard_map(
        shards, mesh=mesh, in_specs=placed, out_specs=P("alpha", "beta"), check_vma=False
    )
```

```python
import functools

import jax
import jax.numpy as jnp
from jax import lax
from jax.experimental import pallas as pl
from jax.experimental.pallas import tpu as pltpu
from jax.sharding import PartitionSpec as P

LANES = 128
BATCH = 32
EARLY = 2
GROUP = 3
NT = (((1,), (1,)), ((), ()))


def stage_kernel(count, *refs):
    sources, (civec_ref, *staged) = refs[: count + 1], refs[count + 1 : 2 * count + 2]
    landing, arrived = refs[2 * count + 2 :]
    copies = [
        pltpu.make_async_copy(source, target, arrived.at[n])
        for n, (source, target) in enumerate(zip(sources, [landing, *staged]))
    ]
    for copy in copies:
        copy.start()
    copies[0].wait()
    civec_ref[...] = landing[...].astype(jnp.bfloat16)
    for copy in copies[1:]:
        copy.wait()


def index_kernel(
    sizes,
    beta_target,
    beta_pair,
    beta_sign,
    alpha_target,
    alpha_pair,
    alpha_sign,
    one_body,
    integrals,
    beta_ref,
    slot_ref,
    alpha_ref,
    weights_ref,
    table,
    turned,
):
    rows, cols, nexc, depth, tiles, pairs = sizes
    bf16, f32 = jnp.bfloat16, jnp.float32
    per_tile = LANES // GROUP
    lane = lax.broadcasted_iota(jnp.int32, (8, LANES), 1)

    h = one_body[...]
    h_high = h.astype(bf16).astype(f32)
    halves = jnp.concatenate([h_high, h - h_high], axis=0)
    table[...] = jnp.zeros_like(table)
    table[pairs + 2 : pairs + 4, :pairs] = halves
    columns = table[...].T
    table[...] = jnp.zeros_like(table)
    table[:pairs, :pairs] = integrals[...].astype(f32)
    table[pairs : pairs + 2, :pairs] = halves
    rows_of = (table[...] + columns).astype(bf16)

    signed = (2 * alpha_sign[...] - 1) * (alpha_pair[...] + 1)
    after = lax.broadcasted_iota(jnp.int32, (depth - nexc, rows), 0) + pairs + 1
    signed = jnp.concatenate([signed, after], axis=0)
    q_ids = lax.broadcasted_iota(jnp.int32, (depth, LANES), 1) + 1
    batch = 16
    for b in range(rows // batch):
        hots = []
        for a in range(b * batch, (b + 1) * batch):
            column = jnp.broadcast_to(signed[:, a : a + 1], (depth, LANES))
            value = jnp.where(column > 0, 1.0, -1.0)
            hots.append(jnp.where(jnp.abs(column) == q_ids, value, 0.0).astype(bf16))
        u = jnp.dot(jnp.concatenate(hots, axis=0), rows_of, preferred_element_type=f32)
        weights_ref[b * batch * depth : (b + 1) * batch * depth, :] = u.astype(bf16)

    code = beta_target[...] * 256 + beta_pair[...] * 2 + beta_sign[...]
    own = lax.axis_index("beta") * cols + lax.broadcasted_iota(jnp.int32, (2, cols), 1)
    extra = lax.broadcasted_iota(jnp.int32, (2, cols), 0) + pairs + 2
    extra = own * 256 + extra * 2 + 1
    blank = jnp.zeros((LANES - nexc - 2, cols), jnp.int32)
    code = jnp.concatenate([code, extra, blank], axis=0).astype(f32)
    turned[...] = jnp.zeros_like(turned)
    for c in range(cols // LANES):
        turned[c * LANES : (c + 1) * LANES, :] = code[:, c * LANES : (c + 1) * LANES].T
    total = jnp.zeros((tiles, LANES), f32)
    for m in range(GROUP):
        part = turned[pl.ds(m, tiles, stride=GROUP), :]
        total += pltpu.roll(part, m * per_tile, 1) if m else part
    total = total.astype(jnp.int32)
    beta_ref[...] = total
    member = lax.div(lax.broadcasted_iota(jnp.int32, (tiles, LANES), 1), per_tile)
    slot = ((total >> 1) & 127) + LANES * member + 1
    slot = jnp.where((total & 1) == 1, slot, -slot).astype(f32)
    turned[:LANES, :] = jnp.zeros((LANES, LANES), f32)
    turned[:tiles, :] = slot
    slot_ref[...] = turned[:LANES, :].T.astype(jnp.int32)

    code = jnp.concatenate(
        [alpha_target[...], jnp.zeros((LANES - nexc, rows), jnp.int32)], axis=0
    )
    turned[:rows, :] = code.astype(f32).T
    period = rows * nexc // LANES // 8
    step = period * LANES // nexc
    found = [jnp.zeros((8, LANES), f32) for w in range(period)]
    for j in range(step):
        part = turned[pl.ds(j, 8, stride=step), :]
        w, shift = divmod(j * nexc, LANES)
        part = pltpu.roll(part, shift, 1) if shift else part
        found[w] += jnp.where(lane >= shift, part, 0.0)
        if shift + nexc > LANES:
            found[w + 1] += jnp.where(lane < shift + nexc - LANES, part, 0.0)
    for w in range(period):
        alpha_ref[8 * w : 8 * w + 8, :] = found[w].astype(jnp.int32)


def scatter(s, first, last, sizes, alpha_ref, lifted):
    rows, nexc = sizes[1], sizes[3]
    base = (lax.axis_index("alpha") ^ s) * rows
    period = rows * nexc // LANES // 8
    b_ids = lax.broadcasted_iota(jnp.int32, (rows, LANES), 0)
    hots = []
    for tile in range(first * nexc // LANES, last * nexc // LANES):
        row = 8 * (tile % period) + tile // period
        target = alpha_ref[row : row + 1, :] - base
        hots.append(jnp.where(b_ids == target, 1.0, 0.0).astype(jnp.bfloat16))
    return jnp.dot(
        jnp.concatenate(hots, axis=1),
        lifted[first * nexc : last * nexc, :],
        preferred_element_type=jnp.float32,
    )


def pick(g, cols, beta_ref, c_refs, first, found):
    code = jnp.concatenate([beta_ref[2 * g : 2 * g + 1], beta_ref[2 * g + 1 : 2 * g + 2]], axis=1)
    target = code >> 8
    low = lax.rem(target, cols)
    high = lax.div(target, cols) ^ lax.axis_index("beta")
    j_ids = lax.broadcasted_iota(jnp.int32, (cols, 2 * LANES), 0)
    hot = jnp.where(j_ids == low, 1.0, 0.0).astype(jnp.bfloat16)
    for k, c_ref in enumerate(c_refs):
        here = jnp.dot(c_ref[...], hot, preferred_element_type=jnp.float32)
        found = here if found is None else jnp.where(high == first + k, here, found)
    return found


def early_kernel(cols, beta_ref, *rest):
    c_refs, early_ref = rest[:-1], rest[-1]
    for g in range(early_ref.shape[0]):
        early_ref[g] = pick(g, cols, beta_ref, c_refs, 0, None).astype(jnp.bfloat16)


def far_kernel(sizes, beta_ref, slot_ref, alpha_ref, weights, early_ref, *rest):
    chunks, rows, cols, nexc, depth, blocks, stride = sizes
    c_refs, rest = rest[: chunks - EARLY], rest[chunks - EARLY :]
    lifted, same = rest[:2]
    out_refs, (density, picked, sums) = rest[2:-3], rest[-3:]
    per_tile = LANES // GROUP
    bf16, f32 = jnp.bfloat16, jnp.float32
    groups = early_ref.shape[0]

    for g in range(groups):
        found = pick(g, cols, beta_ref, c_refs, EARLY, early_ref[g].astype(f32))
        picked[g] = found.astype(bf16)

    ids = lax.broadcasted_iota(jnp.int32, (LANES, LANES), 1) + 1
    for t in range(2 * groups):
        slot = jnp.broadcast_to(slot_ref[:, t : t + 1], (LANES, LANES))
        value = jnp.where(slot > 0, 1.0, -1.0)
        slot = jnp.abs(slot)
        hots = []
        for m in range(GROUP):
            low = m * per_tile // 16 * 16
            high = min(-(-(m + 1) * per_tile // 16) * 16, LANES)
            part = slot[low:high] == ids[low:high] + m * LANES
            part = [jnp.where(part, value[low:high], 0.0).astype(bf16)]
            if low:
                part.insert(0, jnp.zeros((low, LANES), bf16))
            if high < LANES:
                part.append(jnp.zeros((LANES - high, LANES), bf16))
            hots.append(jnp.concatenate(part, axis=0))
        span = slice(t % 2 * LANES, (t % 2 + 1) * LANES)
        d = jnp.dot(
            picked[t // 2, :, span],
            jnp.concatenate(hots, axis=1),
            preferred_element_type=f32,
        )
        for m in range(GROUP):
            i = t * GROUP + m
            density[i * stride : i * stride + rows, :] = d[:, m * LANES : (m + 1) * LANES]

    for first in range(0, rows, BATCH):
        for a in range(first, first + BATCH, 2):
            parts = []
            for m in range(2):
                d = density[pl.ds(a + m, cols, stride=stride), :]
                u = weights[(a + m) * depth : (a + m + 1) * depth, :]
                if m and a % 4:
                    l = lax.dot_general(u, d.astype(bf16), NT, preferred_element_type=f32)
                else:
                    l = jnp.dot(u, d.T.astype(bf16), preferred_element_type=f32)
                same[a + m : a + m + 1, :] = l[nexc : nexc + 1] + l[nexc + 1 : nexc + 2]
                parts.append(l[:nexc])
            lifted[a * nexc : (a + 2) * nexc, :] = jnp.concatenate(parts, axis=0).astype(bf16)
        for s in range(blocks // 2):
            part = scatter(blocks // 2 + s, first, first + BATCH, sizes, alpha_ref, lifted)
            if first:
                part += sums[s]
            if first + BATCH < rows:
                sums[s] = part
            else:
                out_refs[s][...] = part.astype(bf16)


def near_kernel(sizes, alpha_ref, lifted, *out_refs):
    for s, out_ref in enumerate(out_refs):
        total = scatter(s + 1, 0, sizes[1], sizes, alpha_ref, lifted)
        out_ref[...] = total.astype(jnp.bfloat16)


def own_kernel(sizes, alpha_ref, lifted, same, own_ref):
    own_ref[...] = scatter(0, 0, sizes[1], sizes, alpha_ref, lifted) + same[...]


def shards(
    ci_vector,
    one_body,
    pair_integrals,
    beta_target,
    beta_pair,
    beta_sign,
    alpha_target,
    alpha_pair,
    alpha_sign,
):
    rows, cols = ci_vector.shape
    pairs = one_body.shape[0]
    nexc = beta_target.shape[0]
    blocks = lax.axis_size("alpha")
    chunks = lax.axis_size("beta")
    bf16 = jnp.bfloat16

    lists = (
        beta_target,
        beta_pair,
        beta_sign,
        alpha_target,
        alpha_pair,
        alpha_sign,
        one_body.reshape(1, pairs),
        pair_integrals,
    )
    vmem = pl.BlockSpec(memory_space=pltpu.VMEM)
    civec_bf, *lists = pl.pallas_call(
        functools.partial(stage_kernel, len(lists)),
        out_shape=[pltpu.VMEM((rows, cols), bf16)] + [pltpu.VMEM(x.shape, x.dtype) for x in lists],
        in_specs=[pl.BlockSpec(memory_space=pltpu.HBM)] * (1 + len(lists)),
        out_specs=[vmem] * (1 + len(lists)),
        scratch_shapes=[
            pltpu.VMEM((rows, cols), jnp.float32),
            pltpu.SemaphoreType.DMA((1 + len(lists),)),
        ],
        compiler_params=pltpu.CompilerParams(vmem_limit_bytes=4 * 1024 * 1024),
        name="stage",
    )(*[pltpu.with_memory_space_constraint(x, pltpu.HBM) for x in (ci_vector, *lists)])
    gathered = [civec_bf] + [
        lax.ppermute(civec_bf, "beta", [(d, d ^ s) for d in range(chunks)])
        for s in range(1, chunks)
    ]

    depth = nexc + 8
    tiles = -(-cols // (2 * GROUP)) * 2
    beta_code, beta_slot, alpha_code, weights = pl.pallas_call(
        functools.partial(index_kernel, (rows, cols, nexc, depth, tiles, pairs)),
        out_shape=[
            pltpu.VMEM((tiles, LANES), jnp.int32),
            pltpu.VMEM((LANES, LANES), jnp.int32),
            pltpu.VMEM((rows * nexc // LANES, LANES), jnp.int32),
            pltpu.VMEM((rows * depth, LANES), bf16),
        ],
        in_specs=[vmem] * 8,
        out_specs=[vmem] * 4,
        scratch_shapes=[
            pltpu.VMEM((LANES, LANES), jnp.float32),
            pltpu.VMEM((tiles * GROUP, LANES), jnp.float32),
        ],
        cost_estimate=pl.CostEstimate(
            flops=4 * rows * depth * LANES * LANES, bytes_accessed=0, transcendentals=0
        ),
        compiler_params=pltpu.CompilerParams(vmem_limit_bytes=16 * 1024 * 1024),
        name="index_lists",
    )(*lists)

    stride = rows + 4
    early = pl.pallas_call(
        functools.partial(early_kernel, cols),
        out_shape=pltpu.VMEM((tiles // 2, rows, 2 * LANES), bf16),
        in_specs=[vmem] * (1 + EARLY),
        out_specs=vmem,
        compiler_params=pltpu.CompilerParams(vmem_limit_bytes=12 * 1024 * 1024),
        cost_estimate=pl.CostEstimate(
            flops=4 * rows * cols * tiles * LANES, bytes_accessed=0, transcendentals=0
        ),
        name="gather_early",
    )(beta_code, *gathered[:EARLY])
    sizes = (chunks, rows, cols, nexc, depth, blocks, stride)
    block = jax.ShapeDtypeStruct((rows, cols), bf16)
    block_f32 = jax.ShapeDtypeStruct((rows, cols), jnp.float32)
    lifted, same, *far = pl.pallas_call(
        functools.partial(far_kernel, sizes),
        out_shape=[jax.ShapeDtypeStruct((rows * nexc, cols), bf16), block_f32]
        + [block] * (blocks // 2),
        in_specs=[vmem] * (5 + chunks - EARLY),
        out_specs=[vmem] * (2 + blocks // 2),
        scratch_shapes=[
            pltpu.VMEM((tiles * GROUP * stride, LANES), jnp.float32),
            pltpu.VMEM((tiles // 2, rows, 2 * LANES), bf16),
            pltpu.VMEM((blocks // 2, rows, cols), jnp.float32),
        ],
        compiler_params=pltpu.CompilerParams(vmem_limit_bytes=36 * 1024 * 1024),
        name="sigma_far",
    )(beta_code, beta_slot, alpha_code, weights, early, *gathered[EARLY:])

    def send(s, value):
        return lax.ppermute(value, "alpha", [(d, d ^ s) for d in range(blocks)])

    far_sum = far[0].astype(jnp.float32)
    for s in reversed(range(1, blocks // 2)):
        far_sum = far_sum + send(s, far[s]).astype(jnp.float32)
    far_sum = far_sum.astype(bf16)
    near = pl.pallas_call(
        functools.partial(near_kernel, sizes),
        out_shape=[block] * (blocks // 2 - 1),
        in_specs=[vmem] * 2,
        out_specs=[vmem] * (blocks // 2 - 1),
        compiler_params=pltpu.CompilerParams(vmem_limit_bytes=8 * 1024 * 1024),
        cost_estimate=pl.CostEstimate(
            flops=(blocks - 2) * rows * rows * nexc * cols, bytes_accessed=0, transcendentals=0
        ),
        name="sigma_near",
    )(alpha_code, lifted)
    own = pl.pallas_call(
        functools.partial(own_kernel, sizes),
        out_shape=block_f32,
        in_specs=[vmem] * 3,
        out_specs=vmem,
        compiler_params=pltpu.CompilerParams(vmem_limit_bytes=4 * 1024 * 1024),
        cost_estimate=pl.CostEstimate(
            flops=2 * rows * rows * nexc * cols, bytes_accessed=0, transcendentals=0
        ),
        name="sigma_own",
    )(alpha_code, lifted, same)
    crossing = send(blocks // 2, far_sum)
    total = own
    for got in [send(s + 1, near[s]) for s in range(blocks // 2 - 1)] + [crossing]:
        total = total + got.astype(jnp.float32)
    return total


def solution(mesh):
    placed = (
        P("alpha", "beta"),
        P(),
        P(),
        P(None, "beta"),
        P(None, "beta"),
        P(None, "beta"),
        P(None, "alpha"),
        P(None, "alpha"),
        P(None, "alpha"),
    )
    return jax.shard_map(
        shards, mesh=mesh, in_specs=placed, out_specs=P("alpha", "beta"), check_vma=False
    )
```
